512 devices in a mesh: ctx: 16 (over z_lo, x), tp: 32 (over y, z_hi, core).
Axes of the slice: x: 4, y: 4, z: 16 (z_hi: 4, z_lo: 4; z = z_hi * 4 + z_lo), core: 2. Of those that a mesh axis runs over, the one named last changes fastest.
Arguments:
- query_act: bfloat16 [8192, 4096], P('ctx', 'tp'), may hold values from -6 to 6
- key_act: bfloat16 [8192, 4096], P('ctx', 'tp'), may hold values from -6 to 6
- value_act: bfloat16 [8192, 4096], P('ctx', 'tp'), may hold values from -6 to 6
- filter_taps: float32 [8192, 128], P('ctx'), may hold values from -0.06629126 to 0.06629126
- cotangent: bfloat16 [8192, 4096], P('ctx', 'tp'), may hold values from -6 to 6
Outputs:
- gated_out: bfloat16 [8192, 4096], P('ctx', 'tp')
- grad_query: bfloat16 [8192, 4096], P('ctx', 'tp')
- grad_key: bfloat16 [8192, 4096], P('ctx', 'tp')
- grad_value: bfloat16 [8192, 4096], P('ctx', 'tp')
- grad_filter: float32 [8192, 128], P('ctx')
The draws below stay inside these ranges and needn't reach their ends.
All inputs are finite; a program needn't handle non-finite values.
Results may differ from the reference program's by a relative error of at most 0.001.
Values sent between devices are 32-bit elements; how exact they have to be, the bound alone decides.
No kernel may reach another device: no remote copies, remote signals or barrier semaphores. Data moves between devices by JAX's collectives and lax.ppermute only.
A program may use at most 64 MiB of HBM per device.

```python
import math
import jax
import jax.numpy as jnp
from jax import lax

SEQ = 8192
CHANNELS = 4096
FILTERS = 128


def shard_levels(own_key, extent, pieces, low, top_value):
    gain, own = 1.0, jax.random.fold_in(own_key, 6)
    for position, shards_of in pieces:
        draws = jnp.exp(jax.random.uniform(jax.random.fold_in(own, position), (shards_of,), jnp.float32, low / len(pieces), top_value / len(pieces)))
        gain = gain * jnp.repeat(draws, extent[position] // shards_of).reshape([-1 if axis == position else 1 for axis in range(len(extent))])
    return gain


def bell_draw(own_key, extent, scale, most, shards=(), kind=jnp.bfloat16):
    result = scale * jax.random.normal(own_key, extent, jnp.float32)
    if shards:
        result = result * shard_levels(own_key, extent, shards, -0.22, 0.18)
    return jnp.clip(result, -most, most).astype(kind)


def setup_inputs(seed: int = 0) -> dict:
    key_of = jax.random.split(jax.random.key(seed), 6)
    query_act = bell_draw(key_of[0], (SEQ, CHANNELS), 1.0, 6.0, ((0, 16), (1, 32)))
    key_act = bell_draw(key_of[1], (SEQ, CHANNELS), 1.0, 6.0, ((0, 16), (1, 32)))
    value_act = bell_draw(key_of[2], (SEQ, CHANNELS), 1.0, 6.0, ((0, 16), (1, 32)))
    filter_taps = bell_draw(key_of[3], (SEQ, FILTERS), (1.0 / SEQ ** 0.5), 0.06629126, ((0, 16),), jnp.float32)
    cotangent = bell_draw(key_of[4], (SEQ, CHANNELS), 1.0, 6.0, ((0, 16), (1, 32)))
    return {"query_act": query_act, "key_act": key_act, "value_act": value_act, "filter_taps": filter_taps, "cotangent": cotangent}


def reference(query_act, key_act, value_act, filter_taps, cotangent):
    seq_len = query_act.shape[0]
    full_len = 2 * seq_len
    groups = query_act.shape[1] // FILTERS
    filter_spec = jnp.fft.rfft(filter_taps.astype(jnp.float32), n=full_len, axis=0)

    def split_groups(tensor):
        return jnp.transpose(tensor.reshape(seq_len, groups, FILTERS), (1, 0, 2))

    def join_groups(tensor):
        return jnp.transpose(tensor, (1, 0, 2)).reshape(seq_len, groups * FILTERS)

    def one_group(inputs):
        query_rows = inputs[0].astype(jnp.float32)
        key_rows = inputs[1].astype(jnp.float32)
        value_rows = inputs[2].astype(jnp.float32)
        grad_rows = inputs[3].astype(jnp.float32)
        gate_in = key_rows * value_rows
        gate_spec = jnp.fft.rfft(gate_in, n=full_len, axis=0)
        conv_out = jnp.fft.irfft(gate_spec * filter_spec, n=full_len, axis=0)[:seq_len]
        grad_conv = grad_rows * query_rows
        grad_spec = jnp.fft.rfft(grad_conv, n=full_len, axis=0)
        grad_gate = jnp.fft.irfft(grad_spec * jnp.conj(filter_spec), n=full_len, axis=0)[:seq_len]
        filter_terms = jnp.fft.irfft(grad_spec * jnp.conj(gate_spec), n=full_len, axis=0)[:seq_len]
        return ((query_rows * conv_out).astype(jnp.bfloat16), (grad_rows * conv_out).astype(jnp.bfloat16), (grad_gate * value_rows).astype(jnp.bfloat16), (grad_gate * key_rows).astype(jnp.bfloat16), filter_terms.astype(jnp.float32))
    results = lax.map(one_group, (split_groups(query_act), split_groups(key_act), split_groups(value_act), split_groups(cotangent)))
    grad_filter = lax.optimization_barrier(jnp.sum(results[4], axis=0)) / math.sqrt(seq_len * groups)
    return (join_groups(results[0]), join_groups(results[1]), join_groups(results[2]), join_groups(results[3]), grad_filter)
```

```python
import math

import numpy as np
import ml_dtypes
import jax
import jax.numpy as jnp
from jax import lax
from jax.experimental import pallas as pl
from jax.experimental.pallas import tpu as pltpu
from jax.sharding import Mesh, PartitionSpec as P

LANES = 128
GROUP = ("ctx", "y", "core")
PAIRS_NEAR = [(0, 1), (1, 0), (2, 3), (3, 2)]
PAIRS_ROUND = [(0, 3), (3, 0), (1, 2), (2, 1)]


def split_const(table):
    high = table.astype(ml_dtypes.bfloat16)
    low = (table - high.astype(np.float64)).astype(ml_dtypes.bfloat16)
    return high, low


def dft_tables(blocks, chunks):
    first = blocks * chunks
    full = first * LANES
    order = (np.arange(blocks)[None, :] * chunks + np.arange(chunks)[:, None]).reshape(-1)
    k1 = np.arange(first)
    n2 = np.arange(LANES)
    angle = -2 * np.pi * (k1[:, None] * order[None, :] % first) / first + np.pi * order[None, :] / (2 * first)
    first_fwd = np.concatenate([np.cos(angle), np.sin(angle)], 0)
    high, low = split_const(first_fwd)
    first_fwd = np.concatenate([high, high, low], 1)
    high, low = split_const(np.concatenate([np.cos(angle).T, np.sin(angle).T], 1) / full)
    first_inv = np.concatenate([high, high, low], 1)
    angle = -2 * np.pi * (k1[:, None] * n2[None, :]) / full + np.pi * n2[None, :] / (2 * full)
    twist = np.concatenate([np.cos(angle), np.sin(angle)], 1).astype(np.float32)
    angle = 2 * np.pi * (n2[:, None] * n2[None, :] % LANES) / LANES
    cosine, sine = np.cos(angle), np.sin(angle)
    second = np.block([[cosine, -sine], [sine, cosine]])
    second_fwd = np.concatenate(split_const(second), 0)
    second_inv = np.concatenate(split_const(second.T), 0)
    return first_fwd, twist, second_fwd, second_inv, first_inv


def split(values):
    high = values.astype(jnp.bfloat16)
    return high, (values - high.astype(jnp.float32)).astype(jnp.bfloat16)


def dot(left, right):
    return jnp.dot(left, right, preferred_element_type=jnp.float32)


def second_stage(high, low, table):
    table_high = table[: 2 * LANES, :]
    table_low = table[2 * LANES :, :]
    return dot(high, table_high) + dot(low, table_high) + dot(high, table_low)


def pack_kernel(chunks, place_ref, query_ref, key_ref, value_ref, taps_ref, cotangent_ref, send_ref):
    rows = 2 * chunks + 1
    for chunk in range(chunks):
        part = pl.ds(chunk * LANES, LANES)
        gate = key_ref[part, :].astype(jnp.float32) * value_ref[part, :].astype(jnp.float32)
        send_ref[pl.ds(chunk, LANES, stride=rows), :] = gate.T
        grad = query_ref[part, :].astype(jnp.float32) * cotangent_ref[part, :].astype(jnp.float32)
        send_ref[pl.ds(chunks + chunk, LANES, stride=rows), :] = grad.T
    place = place_ref[0]
    start = pl.multiple_of(lax.div(place, 2) * LANES, LANES)
    taps = taps_ref[pl.ds(start, LANES), :].T
    lane = lax.broadcasted_iota(jnp.int32, (LANES, LANES), 1)
    mine = lax.div(lane, LANES // 2) == lax.rem(place, 2)
    send_ref[pl.ds(2 * chunks, LANES, stride=rows), :] = jnp.where(mine, taps, 0.0)


def forward_kernel(
    blocks, chunks, recv_ref, first_ref, twist_ref, second_ref, inverse_ref, first_inv_ref, spec_ref, terms_ref, high_ref, low_ref
):
    rows = 2 * chunks + 1
    first = blocks * chunks
    columns = 2 * chunks
    stride = columns * rows
    cosine = twist_ref[:, :LANES]
    sine = twist_ref[:, LANES:]

    def read(column, signal):
        return jnp.concatenate(
            [recv_ref[pl.ds(column * rows + signal * chunks + chunk, blocks, stride=stride), :] for chunk in range(chunks)], 0
        )

    taps = jnp.concatenate(
        [
            recv_ref[pl.ds(2 * chunk * rows + rows - 1, blocks, stride=stride), :]
            + recv_ref[pl.ds((2 * chunk + 1) * rows + rows - 1, blocks, stride=stride), :]
            for chunk in range(chunks)
        ],
        0,
    )
    signals = [read(column, signal) for signal in range(2) for column in range(columns)] + [taps]
    for start in range(0, len(signals), 2):
        group = signals[start : start + 2]
        wide = jnp.concatenate(group, 1) if len(group) > 1 else group[0]
        high, low = split(wide)
        mixed = dot(first_ref[...], jnp.concatenate([high, low, high], 0))
        for offset in range(len(group)):
            lanes = slice(offset * LANES, (offset + 1) * LANES)
            real, imag = mixed[:first, lanes], mixed[first:, lanes]
            high, low = split(jnp.concatenate([real * cosine - imag * sine, imag * cosine + real * sine], 1))
            place = pl.ds((start + offset) * first, first)
            high_ref[place, :] = high
            low_ref[place, :] = low
    spec_ref[...] = second_stage(high_ref[...], low_ref[...], second_ref)
    real = jnp.zeros((first, LANES), jnp.float32)
    imag = jnp.zeros((first, LANES), jnp.float32)
    for column in range(columns):
        gate = pl.ds(column * first, first)
        grad = pl.ds((columns + column) * first, first)
        gate_real, gate_imag = spec_ref[gate, :LANES], spec_ref[gate, LANES:]
        grad_real, grad_imag = spec_ref[grad, :LANES], spec_ref[grad, LANES:]
        real = real + grad_real * gate_real + grad_imag * gate_imag
        imag = imag + grad_imag * gate_real - grad_real * gate_imag
    high, low = split(jnp.concatenate([real, imag], 1))
    back = second_stage(high, low, inverse_ref)
    real, imag = back[:, :LANES], back[:, LANES:]
    high, low = split(jnp.concatenate([real * cosine + imag * sine, imag * cosine - real * sine], 0))
    terms_ref[...] = dot(first_inv_ref[...], jnp.concatenate([high, low, high], 0))


def inverse_kernel(
    blocks, chunks, spec_ref, terms_ref, more_ref, twist_ref, inverse_ref, first_inv_ref, send_ref, high_ref, low_ref
):
    rows = 3 * chunks
    first = blocks * chunks
    columns = 2 * chunks
    stride = columns * rows
    cosine = twist_ref[:, :LANES]
    sine = twist_ref[:, LANES:]
    taps = pl.ds(2 * columns * first, first)
    taps_real, taps_imag = spec_ref[taps, :LANES], spec_ref[taps, LANES:]
    for column in range(columns):
        place = pl.ds(column * first, first)
        real, imag = spec_ref[place, :LANES], spec_ref[place, LANES:]
        high, low = split(jnp.concatenate([real * taps_real - imag * taps_imag, real * taps_imag + imag * taps_real], 1))
        high_ref[place, :] = high
        low_ref[place, :] = low
        place = pl.ds((columns + column) * first, first)
        real, imag = spec_ref[place, :LANES], spec_ref[place, LANES:]
        high, low = split(jnp.concatenate([real * taps_real + imag * taps_imag, imag * taps_real - real * taps_imag], 1))
        high_ref[place, :] = high
        low_ref[place, :] = low
    back = second_stage(high_ref[...], low_ref[...], inverse_ref)
    for signal in range(2):
        for column in range(0, columns, 2):
            sides = []
            for offset in range(2):
                begin = (signal * columns + column + offset) * first
                real, imag = back[begin : begin + first, :LANES], back[begin : begin + first, LANES:]
                sides.append(jnp.concatenate([real * cosine + imag * sine, imag * cosine - real * sine], 0))
            high, low = split(jnp.concatenate(sides, 1))
            result = dot(first_inv_ref[...], jnp.concatenate([high, low, high], 0))
            for offset in range(2):
                for chunk in range(chunks):
                    send_ref[pl.ds((column + offset) * rows + signal * chunks + chunk, blocks, stride=stride), :] = result[
                        chunk * blocks : (chunk + 1) * blocks, offset * LANES : (offset + 1) * LANES
                    ]
    total = terms_ref[...] + more_ref[...]
    for chunk in range(chunks):
        piece = total[chunk * blocks : (chunk + 1) * blocks, :]
        for column in range(columns):
            send_ref[pl.ds(column * rows + 2 * chunks + chunk, blocks, stride=stride), :] = piece


def output_kernel(
    chunks, scale, recv_ref, query_ref, key_ref, value_ref, cotangent_ref,
    gated_ref, grad_query_ref, grad_key_ref, grad_value_ref, grad_taps_ref,
):
    rows = 3 * chunks
    for chunk in range(chunks):
        part = pl.ds(chunk * LANES, LANES)
        conv = recv_ref[pl.ds(chunk, LANES, stride=rows), :].T
        gated_ref[part, :] = (query_ref[part, :].astype(jnp.float32) * conv).astype(jnp.bfloat16)
        grad_query_ref[part, :] = (cotangent_ref[part, :].astype(jnp.float32) * conv).astype(jnp.bfloat16)
        grad_gate = recv_ref[pl.ds(chunks + chunk, LANES, stride=rows), :].T
        grad_key_ref[part, :] = (grad_gate * value_ref[part, :].astype(jnp.float32)).astype(jnp.bfloat16)
        grad_value_ref[part, :] = (grad_gate * key_ref[part, :].astype(jnp.float32)).astype(jnp.bfloat16)
        grad_taps_ref[part, :] = recv_ref[pl.ds(2 * chunks + chunk, LANES, stride=rows), :].T * scale


def params():
    return pltpu.CompilerParams(vmem_limit_bytes=48 * 1024 * 1024)


def whole(count):
    return [pl.BlockSpec(memory_space=pltpu.VMEM)] * count


def pack(place, query, key, value, taps, cotangent):
    length = query.shape[0]
    chunks = length // LANES
    return pl.pallas_call(
        lambda *refs: pack_kernel(chunks, *refs),
        out_shape=jax.ShapeDtypeStruct((LANES * (2 * chunks + 1), LANES), jnp.float32),
        in_specs=[pl.BlockSpec(memory_space=pltpu.SMEM)] + whole(5),
        out_specs=whole(1)[0],
        compiler_params=params(),
        name="pack",
    )(place, query, key, value, taps, cotangent)


def forward(blocks, chunks, recv, first_fwd, twist, second_fwd, second_inv, first_inv):
    first = blocks * chunks
    count = (4 * chunks + 1) * first
    return pl.pallas_call(
        lambda *refs: forward_kernel(blocks, chunks, *refs),
        out_shape=(
            jax.ShapeDtypeStruct((count, 2 * LANES), jnp.float32),
            jax.ShapeDtypeStruct((first, LANES), jnp.float32),
        ),
        in_specs=whole(6),
        out_specs=tuple(whole(2)),
        scratch_shapes=[pltpu.VMEM((count, 2 * LANES), jnp.bfloat16)] * 2,
        compiler_params=params(),
        name="forward",
    )(recv, first_fwd, twist, second_fwd, second_inv, first_inv)


def inverse(blocks, chunks, spec, terms, more, twist, second_inv, first_inv):
    count = 4 * chunks * blocks * chunks
    return pl.pallas_call(
        lambda *refs: inverse_kernel(blocks, chunks, *refs),
        out_shape=jax.ShapeDtypeStruct((LANES * 3 * chunks, LANES), jnp.float32),
        in_specs=whole(6),
        out_specs=whole(1)[0],
        scratch_shapes=[pltpu.VMEM((count, 2 * LANES), jnp.bfloat16)] * 2,
        compiler_params=params(),
        name="inverse",
    )(spec, terms, more, twist, second_inv, first_inv)


def outputs(scale, recv, query, key, value, cotangent):
    length = query.shape[0]
    chunks = length // LANES
    rows = jax.ShapeDtypeStruct((length, LANES), jnp.bfloat16)
    return pl.pallas_call(
        lambda *refs: output_kernel(chunks, scale, *refs),
        out_shape=(rows, rows, rows, rows, jax.ShapeDtypeStruct((length, LANES), jnp.float32)),
        in_specs=whole(5),
        out_specs=tuple(whole(5)),
        compiler_params=params(),
        name="outputs",
    )(recv, query, key, value, cotangent)


def exchange(rows):
    shape = rows.shape
    flat = rows.reshape(LANES, 1, -1)
    return lax.all_to_all(flat, GROUP, 0, 0, tiled=True).reshape(shape)


def on_device(query, key, value, taps, cotangent):
    blocks = lax.axis_size("ctx")
    length = query.shape[0]
    chunks = length // LANES
    first_fwd, twist, second_fwd, second_inv, first_inv = (
        jnp.asarray(table) for table in dft_tables(blocks, chunks)
    )
    place = lax.axis_index(("y", "core")).astype(jnp.int32).reshape(1)
    recv = exchange(pack(place, query, key, value, taps, cotangent))
    spec, terms = forward(blocks, chunks, recv, first_fwd, twist, second_fwd, second_inv, first_inv)
    terms = terms + lax.ppermute(terms, "zh", PAIRS_NEAR)
    more = lax.ppermute(terms, "zh", PAIRS_ROUND)
    back = exchange(inverse(blocks, chunks, spec, terms, more, twist, second_inv, first_inv))
    scale = 1.0 / math.sqrt(float(blocks * length * lax.axis_size(("y", "zh", "core"))))
    return outputs(scale, back, query, key, value, cotangent)


def solution(mesh):
    split_mesh = Mesh(mesh.devices.reshape(mesh.shape["ctx"], 4, 4, 2), ("ctx", "y", "zh", "core"))
    tp = ("y", "zh", "core")
    wide = P("ctx", tp)
    return jax.shard_map(
        on_device,
        mesh=split_mesh,
        in_specs=(wide, wide, wide, P("ctx", None), wide),
        out_specs=(wide, wide, wide, wide, P("ctx", None)),
        check_vma=False,
    )
```

```python
import math

import numpy as np
import ml_dtypes
import jax
import jax.numpy as jnp
from jax import lax
from jax.experimental import pallas as pl
from jax.experimental.pallas import tpu as pltpu
from jax.sharding import Mesh, PartitionSpec as P

LANES = 128
GROUP = ("ctx", "y", "core")
PAIRS_NEAR = [(0, 1), (1, 0), (2, 3), (3, 2)]
PAIRS_ROUND = [(0, 3), (3, 0), (1, 2), (2, 1)]


def split_const(table):
    high = table.astype(ml_dtypes.bfloat16)
    low = (table - high.astype(np.float64)).astype(ml_dtypes.bfloat16)
    return high, low


def dft_tables(blocks, chunks):
    first = blocks * chunks
    full = first * LANES
    order = (np.arange(blocks)[None, :] * chunks + np.arange(chunks)[:, None]).reshape(-1)
    k1 = np.arange(first)
    n2 = np.arange(LANES)
    angle = -2 * np.pi * (k1[:, None] * order[None, :] % first) / first + np.pi * order[None, :] / (2 * first)
    first_fwd = np.concatenate([np.cos(angle), np.sin(angle)], 0)
    high, low = split_const(first_fwd)
    first_fwd = np.concatenate([high, high, low], 1)
    high, low = split_const(np.concatenate([np.cos(angle).T, np.sin(angle).T], 1) / full)
    first_inv = np.concatenate([high, high, low], 1)
    angle = -2 * np.pi * (k1[:, None] * n2[None, :]) / full + np.pi * n2[None, :] / (2 * full)
    twist = np.concatenate([np.cos(angle), np.sin(angle)], 1).astype(np.float32)
    angle = 2 * np.pi * (n2[:, None] * n2[None, :] % LANES) / LANES
    cosine, sine = np.cos(angle), np.sin(angle)
    second = np.block([[cosine, -sine], [sine, cosine]])
    second_fwd = np.concatenate(split_const(second), 0)
    second_inv = np.concatenate(split_const(second.T), 0)
    return first_fwd, twist, second_fwd, second_inv, first_inv


def split(values):
    high = values.astype(jnp.bfloat16)
    return high, (values - high.astype(jnp.float32)).astype(jnp.bfloat16)


def dot(left, right):
    return jnp.dot(left, right, preferred_element_type=jnp.float32)


def second_stage(high, low, table):
    table_high = table[: 2 * LANES, :]
    table_low = table[2 * LANES :, :]
    return dot(high, table_high) + dot(low, table_high) + dot(high, table_low)


def pack_kernel(
    chunks, place_ref, query_hbm, key_hbm, value_hbm, taps_hbm, cotangent_hbm, send_ref,
    query_ref, key_ref, value_ref, taps_ref, cotangent_ref, done_ref,
):
    rows = 2 * chunks + 1
    place = place_ref[0]
    start = pl.multiple_of(lax.div(place, 2) * LANES, LANES)
    pairs = (
        (key_hbm, key_ref),
        (value_hbm, value_ref),
        (query_hbm, query_ref),
        (cotangent_hbm, cotangent_ref),
        (taps_hbm.at[pl.ds(start, LANES), :], taps_ref),
    )
    copies = [pltpu.make_async_copy(source, target, done_ref.at[n]) for n, (source, target) in enumerate(pairs)]
    for copy in copies:
        copy.start()
    copies[0].wait()
    copies[1].wait()
    for chunk in range(chunks):
        part = pl.ds(chunk * LANES, LANES)
        gate = key_ref[part, :].astype(jnp.float32) * value_ref[part, :].astype(jnp.float32)
        send_ref[pl.ds(chunk, LANES, stride=rows), :] = gate.T
    copies[2].wait()
    copies[3].wait()
    for chunk in range(chunks):
        part = pl.ds(chunk * LANES, LANES)
        grad = query_ref[part, :].astype(jnp.float32) * cotangent_ref[part, :].astype(jnp.float32)
        send_ref[pl.ds(chunks + chunk, LANES, stride=rows), :] = grad.T
    copies[4].wait()
    lane = lax.broadcasted_iota(jnp.int32, (LANES, LANES), 1)
    mine = lax.div(lane, LANES // 2) == lax.rem(place, 2)
    send_ref[pl.ds(2 * chunks, LANES, stride=rows), :] = jnp.where(mine, taps_ref[...].T, 0.0)


def forward_kernel(
    blocks, chunks, recv_ref, first_ref, twist_ref, second_ref, inverse_ref, first_inv_ref, spec_ref, terms_ref, high_ref, low_ref
):
    rows = 2 * chunks + 1
    first = blocks * chunks
    columns = 2 * chunks
    stride = columns * rows
    cosine = twist_ref[:, :LANES]
    sine = twist_ref[:, LANES:]

    def read(column, signal):
        return jnp.concatenate(
            [recv_ref[pl.ds(column * rows + signal * chunks + chunk, blocks, stride=stride), :] for chunk in range(chunks)], 0
        )

    taps = jnp.concatenate(
        [
            recv_ref[pl.ds(2 * chunk * rows + rows - 1, blocks, stride=stride), :]
            + recv_ref[pl.ds((2 * chunk + 1) * rows + rows - 1, blocks, stride=stride), :]
            for chunk in range(chunks)
        ],
        0,
    )
    signals = [read(column, signal) for signal in range(2) for column in range(columns)] + [taps]
    for start in range(0, len(signals), 2):
        group = signals[start : start + 2]
        wide = jnp.concatenate(group, 1) if len(group) > 1 else group[0]
        high, low = split(wide)
        mixed = dot(first_ref[...], jnp.concatenate([high, low, high], 0))
        for offset in range(len(group)):
            lanes = slice(offset * LANES, (offset + 1) * LANES)
            real, imag = mixed[:first, lanes], mixed[first:, lanes]
            high, low = split(jnp.concatenate([real * cosine - imag * sine, imag * cosine + real * sine], 1))
            place = pl.ds((start + offset) * first, first)
            high_ref[place, :] = high
            low_ref[place, :] = low
    spec_ref[...] = second_stage(high_ref[...], low_ref[...], second_ref)
    real = jnp.zeros((first, LANES), jnp.float32)
    imag = jnp.zeros((first, LANES), jnp.float32)
    for column in range(columns):
        gate = pl.ds(column * first, first)
        grad = pl.ds((columns + column) * first, first)
        gate_real, gate_imag = spec_ref[gate, :LANES], spec_ref[gate, LANES:]
        grad_real, grad_imag = spec_ref[grad, :LANES], spec_ref[grad, LANES:]
        real = real + grad_real * gate_real + grad_imag * gate_imag
        imag = imag + grad_imag * gate_real - grad_real * gate_imag
    high, low = split(jnp.concatenate([real, imag], 1))
    back = second_stage(high, low, inverse_ref)
    real, imag = back[:, :LANES], back[:, LANES:]
    high, low = split(jnp.concatenate([real * cosine + imag * sine, imag * cosine - real * sine], 0))
    terms_ref[...] = dot(first_inv_ref[...], jnp.concatenate([high, low, high], 0))


def inverse_kernel(blocks, chunks, spec_ref, twist_ref, inverse_ref, first_inv_ref, send_ref, high_ref, low_ref):
    first = blocks * chunks
    columns = 2 * chunks
    cosine = twist_ref[:, :LANES]
    sine = twist_ref[:, LANES:]
    taps = pl.ds(2 * columns * first, first)
    taps_real, taps_imag = spec_ref[taps, :LANES], spec_ref[taps, LANES:]
    for column in range(columns):
        place = pl.ds(column * first, first)
        real, imag = spec_ref[place, :LANES], spec_ref[place, LANES:]
        high, low = split(jnp.concatenate([real * taps_real - imag * taps_imag, real * taps_imag + imag * taps_real], 1))
        high_ref[place, :] = high
        low_ref[place, :] = low
        place = pl.ds((columns + column) * first, first)
        real, imag = spec_ref[place, :LANES], spec_ref[place, LANES:]
        high, low = split(jnp.concatenate([real * taps_real + imag * taps_imag, imag * taps_real - real * taps_imag], 1))
        high_ref[place, :] = high
        low_ref[place, :] = low
    rows = 3 * chunks
    stride = columns * rows
    back = second_stage(high_ref[...], low_ref[...], inverse_ref)
    for signal in range(2):
        for column in range(0, columns, 2):
            sides = []
            for offset in range(2):
                begin = (signal * columns + column + offset) * first
                real, imag = back[begin : begin + first, :LANES], back[begin : begin + first, LANES:]
                sides.append(jnp.concatenate([real * cosine + imag * sine, imag * cosine - real * sine], 0))
            high, low = split(jnp.concatenate(sides, 1))
            result = dot(first_inv_ref[...], jnp.concatenate([high, low, high], 0))
            for offset in range(2):
                for chunk in range(chunks):
                    send_ref[pl.ds((column + offset) * rows + signal * chunks + chunk, blocks, stride=stride), :] = result[
                        chunk * blocks : (chunk + 1) * blocks, offset * LANES : (offset + 1) * LANES
                    ]


def fill_kernel(blocks, chunks, count, send_in_ref, *refs):
    columns = 2 * chunks
    rows = 3 * chunks
    total = refs[0][...]
    for ref in refs[1:count]:
        total = total + ref[...]
    send_ref = refs[count]
    for chunk in range(chunks):
        piece = total[chunk * blocks : (chunk + 1) * blocks, :]
        for column in range(columns):
            send_ref[pl.ds(column * rows + 2 * chunks + chunk, blocks, stride=columns * rows), :] = piece


def output_kernel(
    chunks, scale, recv_ref, query_ref, key_ref, value_ref, cotangent_ref,
    gated_ref, grad_query_ref, grad_key_ref, grad_value_ref, grad_taps_ref,
):
    rows = 3 * chunks
    for chunk in range(chunks):
        part = pl.ds(chunk * LANES, LANES)
        conv = recv_ref[pl.ds(chunk, LANES, stride=rows), :].T
        gated_ref[part, :] = (query_ref[part, :].astype(jnp.float32) * conv).astype(jnp.bfloat16)
        grad_query_ref[part, :] = (cotangent_ref[part, :].astype(jnp.float32) * conv).astype(jnp.bfloat16)
        grad_gate = recv_ref[pl.ds(chunks + chunk, LANES, stride=rows), :].T
        grad_key_ref[part, :] = (grad_gate * value_ref[part, :].astype(jnp.float32)).astype(jnp.bfloat16)
        grad_value_ref[part, :] = (grad_gate * key_ref[part, :].astype(jnp.float32)).astype(jnp.bfloat16)
        grad_taps_ref[part, :] = recv_ref[pl.ds(2 * chunks + chunk, LANES, stride=rows), :].T * scale


def params():
    return pltpu.CompilerParams(vmem_limit_bytes=48 * 1024 * 1024)


def whole(count):
    return [pl.BlockSpec(memory_space=pltpu.VMEM)] * count


def pack(place, query, key, value, taps, cotangent):
    length = query.shape[0]
    chunks = length // LANES
    wide = pltpu.VMEM((length, LANES), jnp.bfloat16)
    return pl.pallas_call(
        lambda *refs: pack_kernel(chunks, *refs),
        out_shape=jax.ShapeDtypeStruct((LANES * (2 * chunks + 1), LANES), jnp.float32),
        in_specs=[pl.BlockSpec(memory_space=pltpu.SMEM)] + [pl.BlockSpec(memory_space=pltpu.HBM)] * 5,
        out_specs=whole(1)[0],
        scratch_shapes=[wide, wide, wide, pltpu.VMEM((LANES, LANES), jnp.float32), wide, pltpu.SemaphoreType.DMA((5,))],
        compiler_params=params(),
        name="pack",
    )(place, *(pltpu.with_memory_space_constraint(array, pltpu.HBM) for array in (query, key, value, taps, cotangent)))


def forward(blocks, chunks, recv, first_fwd, twist, second_fwd, second_inv, first_inv):
    first = blocks * chunks
    count = (4 * chunks + 1) * first
    return pl.pallas_call(
        lambda *refs: forward_kernel(blocks, chunks, *refs),
        out_shape=(
            jax.ShapeDtypeStruct((count, 2 * LANES), jnp.float32),
            jax.ShapeDtypeStruct((first, LANES), jnp.float32),
        ),
        in_specs=whole(6),
        out_specs=tuple(whole(2)),
        scratch_shapes=[pltpu.VMEM((count, 2 * LANES), jnp.bfloat16)] * 2,
        compiler_params=params(),
        name="forward",
    )(recv, first_fwd, twist, second_fwd, second_inv, first_inv)


def inverse(blocks, chunks, spec, twist, second_inv, first_inv):
    count = 4 * chunks * blocks * chunks
    return pl.pallas_call(
        lambda *refs: inverse_kernel(blocks, chunks, *refs),
        out_shape=jax.ShapeDtypeStruct((LANES * 3 * chunks, LANES), jnp.float32),
        in_specs=whole(4),
        out_specs=whole(1)[0],
        scratch_shapes=[pltpu.VMEM((count, 2 * LANES), jnp.bfloat16)] * 2,
        compiler_params=params(),
        cost_estimate=pl.CostEstimate(flops=10**9, bytes_accessed=4 * 10**6, transcendentals=0),
        name="inverse",
    )(spec, twist, second_inv, first_inv)


def fill(blocks, chunks, send, *terms):
    return pl.pallas_call(
        lambda *refs: fill_kernel(blocks, chunks, len(terms), *refs),
        out_shape=jax.ShapeDtypeStruct(send.shape, jnp.float32),
        in_specs=whole(1 + len(terms)),
        out_specs=whole(1)[0],
        input_output_aliases={0: 0},
        compiler_params=params(),
        name="fill",
    )(send, *terms)


def outputs(scale, recv, query, key, value, cotangent):
    length = query.shape[0]
    chunks = length // LANES
    rows = jax.ShapeDtypeStruct((length, LANES), jnp.bfloat16)
    return pl.pallas_call(
        lambda *refs: output_kernel(chunks, scale, *refs),
        out_shape=(rows, rows, rows, rows, jax.ShapeDtypeStruct((length, LANES), jnp.float32)),
        in_specs=whole(5),
        out_specs=tuple(whole(5)),
        compiler_params=params(),
        name="outputs",
    )(recv, query, key, value, cotangent)


def exchange(rows):
    shape = rows.shape
    flat = rows.reshape(LANES, 1, -1)
    return lax.all_to_all(flat, GROUP, 0, 0, tiled=True).reshape(shape)


def on_device(query, key, value, taps, cotangent):
    blocks = lax.axis_size("ctx")
    length = query.shape[0]
    chunks = length // LANES
    first_fwd, twist, second_fwd, second_inv, first_inv = (
        jnp.asarray(table) for table in dft_tables(blocks, chunks)
    )
    place = lax.axis_index(("y", "core")).astype(jnp.int32).reshape(1)
    recv = exchange(pack(place, query, key, value, taps, cotangent))
    spec, terms = forward(blocks, chunks, recv, first_fwd, twist, second_fwd, second_inv, first_inv)
    send = inverse(blocks, chunks, spec, twist, second_inv, first_inv)
    terms = terms + lax.ppermute(terms, "zh", PAIRS_NEAR)
    send = fill(blocks, chunks, send, terms, lax.ppermute(terms, "zh", PAIRS_ROUND))
    back = exchange(send)
    scale = 1.0 / math.sqrt(float(blocks * length * lax.axis_size(("y", "zh", "core"))))
    return outputs(scale, back, query, key, value, cotangent)


def solution(mesh):
    split_mesh = Mesh(mesh.devices.reshape(mesh.shape["ctx"], 4, 4, 2), ("ctx", "y", "zh", "core"))
    tp = ("y", "zh", "core")
    wide = P("ctx", tp)
    return jax.shard_map(
        on_device,
        mesh=split_mesh,
        in_specs=(wide, wide, wide, P("ctx", None), wide),
        out_specs=(wide, wide, wide, wide, P("ctx", None)),
        check_vma=False,
    )
```

```python
import math

import numpy as np
import ml_dtypes
import jax
import jax.numpy as jnp
from jax import lax
from jax.experimental import pallas as pl
from jax.experimental.pallas import tpu as pltpu
from jax.sharding import Mesh, PartitionSpec as P

LANES = 128
GROUP = ("ctx", "y", "core")
PAIRS_NEAR = [(0, 1), (1, 0), (2, 3), (3, 2)]
PAIRS_ROUND = [(0, 3), (3, 0), (1, 2), (2, 1)]


def split_const(table):
    high = table.astype(ml_dtypes.bfloat16)
    low = (table - high.astype(np.float64)).astype(ml_dtypes.bfloat16)
    return high, low


def dft_tables(blocks, chunks):
    first = blocks * chunks
    full = first * LANES
    order = (np.arange(blocks)[None, :] * chunks + np.arange(chunks)[:, None]).reshape(-1)
    k1 = np.arange(first)
    n2 = np.arange(LANES)
    angle = -2 * np.pi * (k1[:, None] * order[None, :] % first) / first + np.pi * order[None, :] / (2 * first)
    first_fwd = np.concatenate([np.cos(angle), np.sin(angle)], 0)
    high, low = split_const(first_fwd)
    first_fwd = np.concatenate([high, high, low], 1)
    high, low = split_const(np.concatenate([np.cos(angle).T, np.sin(angle).T], 1) / full)
    first_inv = np.concatenate([high, high, low], 1)
    angle = -2 * np.pi * (k1[:, None] * n2[None, :]) / full + np.pi * n2[None, :] / (2 * full)
    twist = np.concatenate([np.cos(angle), np.sin(angle)], 1).astype(np.float32)
    angle = 2 * np.pi * (n2[:, None] * n2[None, :] % LANES) / LANES
    cosine, sine = np.cos(angle), np.sin(angle)
    second = np.block([[cosine, -sine], [sine, cosine]])
    second_fwd = np.concatenate(split_const(second), 0)
    second_inv = np.concatenate(split_const(second.T), 0)
    return first_fwd, twist, second_fwd, second_inv, first_inv


def split(values):
    high = values.astype(jnp.bfloat16)
    return high, (values - high.astype(jnp.float32)).astype(jnp.bfloat16)


def dot(left, right):
    return jnp.dot(left, right, preferred_element_type=jnp.float32)


def second_stage(high, low, table):
    table_high = table[: 2 * LANES, :]
    table_low = table[2 * LANES :, :]
    return dot(high, table_high) + dot(low, table_high) + dot(high, table_low)


def pack_kernel(
    chunks, place_ref, query_hbm, key_hbm, value_hbm, taps_hbm, cotangent_hbm, send_ref,
    query_ref, key_ref, value_ref, taps_ref, cotangent_ref, done_ref,
):
    rows = 2 * chunks + 1
    place = place_ref[0]
    start = pl.multiple_of(lax.div(place, 2) * LANES, LANES)
    pairs = (
        (key_hbm, key_ref),
        (value_hbm, value_ref),
        (query_hbm, query_ref),
        (cotangent_hbm, cotangent_ref),
        (taps_hbm.at[pl.ds(start, LANES), :], taps_ref),
    )
    copies = [pltpu.make_async_copy(source, target, done_ref.at[n]) for n, (source, target) in enumerate(pairs)]
    for copy in copies:
        copy.start()
    copies[0].wait()
    copies[1].wait()
    for chunk in range(chunks):
        part = pl.ds(chunk * LANES, LANES)
        gate = key_ref[part, :].astype(jnp.float32) * value_ref[part, :].astype(jnp.float32)
        send_ref[pl.ds(chunk, LANES, stride=rows), :] = gate.T
    copies[2].wait()
    copies[3].wait()
    for chunk in range(chunks):
        part = pl.ds(chunk * LANES, LANES)
        grad = query_ref[part, :].astype(jnp.float32) * cotangent_ref[part, :].astype(jnp.float32)
        send_ref[pl.ds(chunks + chunk, LANES, stride=rows), :] = grad.T
    copies[4].wait()
    lane = lax.broadcasted_iota(jnp.int32, (LANES, LANES), 1)
    mine = lax.div(lane, LANES // 2) == lax.rem(place, 2)
    send_ref[pl.ds(2 * chunks, LANES, stride=rows), :] = jnp.where(mine, taps_ref[...].T, 0.0)


def forward_kernel(
    blocks, chunks, recv_ref, first_ref, twist_ref, second_ref, inverse_ref, first_inv_ref, spec_ref, terms_ref, high_ref, low_ref
):
    rows = 2 * chunks + 1
    first = blocks * chunks
    columns = 2 * chunks
    stride = columns * rows
    cosine = twist_ref[:, :LANES]
    sine = twist_ref[:, LANES:]

    def read(column, signal):
        return jnp.concatenate(
            [recv_ref[pl.ds(column * rows + signal * chunks + chunk, blocks, stride=stride), :] for chunk in range(chunks)], 0
        )

    taps = jnp.concatenate(
        [
            recv_ref[pl.ds(2 * chunk * rows + rows - 1, blocks, stride=stride), :]
            + recv_ref[pl.ds((2 * chunk + 1) * rows + rows - 1, blocks, stride=stride), :]
            for chunk in range(chunks)
        ],
        0,
    )
    signals = [read(column, signal) for signal in range(2) for column in range(columns)] + [taps]
    for start in range(0, len(signals), 2):
        group = signals[start : start + 2]
        wide = jnp.concatenate(group, 1) if len(group) > 1 else group[0]
        high, low = split(wide)
        mixed = dot(first_ref[...], jnp.concatenate([high, low, high], 0))
        for offset in range(len(group)):
            lanes = slice(offset * LANES, (offset + 1) * LANES)
            real, imag = mixed[:first, lanes], mixed[first:, lanes]
            high, low = split(jnp.concatenate([real * cosine - imag * sine, imag * cosine + real * sine], 1))
            place = pl.ds((start + offset) * first, first)
            high_ref[place, :] = high
            low_ref[place, :] = low
    spec_ref[...] = second_stage(high_ref[...], low_ref[...], second_ref)
    real = jnp.zeros((first, LANES), jnp.float32)
    imag = jnp.zeros((first, LANES), jnp.float32)
    for column in range(columns):
        gate = pl.ds(column * first, first)
        grad = pl.ds((columns + column) * first, first)
        gate_real, gate_imag = spec_ref[gate, :LANES], spec_ref[gate, LANES:]
        grad_real, grad_imag = spec_ref[grad, :LANES], spec_ref[grad, LANES:]
        real = real + grad_real * gate_real + grad_imag * gate_imag
        imag = imag + grad_imag * gate_real - grad_real * gate_imag
    high, low = split(jnp.concatenate([real, imag], 1))
    back = second_stage(high, low, inverse_ref)
    real, imag = back[:, :LANES], back[:, LANES:]
    high, low = split(jnp.concatenate([real * cosine + imag * sine, imag * cosine - real * sine], 0))
    terms_ref[...] = dot(first_inv_ref[...], jnp.concatenate([high, low, high], 0))


def inverse_kernel(blocks, chunks, spec_ref, twist_ref, inverse_ref, first_inv_ref, send_ref, high_ref, low_ref):
    first = blocks * chunks
    columns = 2 * chunks
    cosine = twist_ref[:, :LANES]
    sine = twist_ref[:, LANES:]
    taps = pl.ds(2 * columns * first, first)
    taps_real, taps_imag = spec_ref[taps, :LANES], spec_ref[taps, LANES:]
    for column in range(columns):
        place = pl.ds(column * first, first)
        real, imag = spec_ref[place, :LANES], spec_ref[place, LANES:]
        high, low = split(jnp.concatenate([real * taps_real - imag * taps_imag, real * taps_imag + imag * taps_real], 1))
        high_ref[place, :] = high
        low_ref[place, :] = low
        place = pl.ds((columns + column) * first, first)
        real, imag = spec_ref[place, :LANES], spec_ref[place, LANES:]
        high, low = split(jnp.concatenate([real * taps_real + imag * taps_imag, imag * taps_real - real * taps_imag], 1))
        high_ref[place, :] = high
        low_ref[place, :] = low
    rows = 2 * chunks
    stride = columns * rows
    back = second_stage(high_ref[...], low_ref[...], inverse_ref)
    for signal in range(2):
        for column in range(0, columns, 2):
            sides = []
            for offset in range(2):
                begin = (signal * columns + column + offset) * first
                real, imag = back[begin : begin + first, :LANES], back[begin : begin + first, LANES:]
                sides.append(jnp.concatenate([real * cosine + imag * sine, imag * cosine - real * sine], 0))
            high, low = split(jnp.concatenate(sides, 1))
            result = dot(first_inv_ref[...], jnp.concatenate([high, low, high], 0))
            for offset in range(2):
                for chunk in range(chunks):
                    send_ref[pl.ds((column + offset) * rows + signal * chunks + chunk, blocks, stride=stride), :] = result[
                        chunk * blocks : (chunk + 1) * blocks, offset * LANES : (offset + 1) * LANES
                    ]


def fill_kernel(blocks, chunks, count, conv_ref, *refs):
    columns = 2 * chunks
    rows = 3 * chunks
    total = refs[0][...]
    for ref in refs[1:count]:
        total = total + ref[...]
    send_ref = refs[count]
    for place in range(blocks * columns):
        send_ref[pl.ds(place * rows, 2 * chunks), :] = conv_ref[pl.ds(place * 2 * chunks, 2 * chunks), :]
    for chunk in range(chunks):
        piece = total[chunk * blocks : (chunk + 1) * blocks, :]
        for column in range(columns):
            send_ref[pl.ds(column * rows + 2 * chunks + chunk, blocks, stride=columns * rows), :] = piece


def output_kernel(
    chunks, scale, recv_ref, query_ref, key_ref, value_ref, cotangent_ref,
    gated_ref, grad_query_ref, grad_key_ref, grad_value_ref, grad_taps_ref,
):
    rows = 3 * chunks
    for chunk in range(chunks):
        part = pl.ds(chunk * LANES, LANES)
        conv = recv_ref[pl.ds(chunk, LANES, stride=rows), :].T
        gated_ref[part, :] = (query_ref[part, :].astype(jnp.float32) * conv).astype(jnp.bfloat16)
        grad_query_ref[part, :] = (cotangent_ref[part, :].astype(jnp.float32) * conv).astype(jnp.bfloat16)
        grad_gate = recv_ref[pl.ds(chunks + chunk, LANES, stride=rows), :].T
        grad_key_ref[part, :] = (grad_gate * value_ref[part, :].astype(jnp.float32)).astype(jnp.bfloat16)
        grad_value_ref[part, :] = (grad_gate * key_ref[part, :].astype(jnp.float32)).astype(jnp.bfloat16)
        grad_taps_ref[part, :] = recv_ref[pl.ds(2 * chunks + chunk, LANES, stride=rows), :].T * scale


def params():
    return pltpu.CompilerParams(vmem_limit_bytes=48 * 1024 * 1024)


def whole(count):
    return [pl.BlockSpec(memory_space=pltpu.VMEM)] * count


def pack(place, query, key, value, taps, cotangent):
    length = query.shape[0]
    chunks = length // LANES
    wide = pltpu.VMEM((length, LANES), jnp.bfloat16)
    return pl.pallas_call(
        lambda *refs: pack_kernel(chunks, *refs),
        out_shape=jax.ShapeDtypeStruct((LANES * (2 * chunks + 1), LANES), jnp.float32),
        in_specs=[pl.BlockSpec(memory_space=pltpu.SMEM)] + [pl.BlockSpec(memory_space=pltpu.HBM)] * 5,
        out_specs=whole(1)[0],
        scratch_shapes=[wide, wide, wide, pltpu.VMEM((LANES, LANES), jnp.float32), wide, pltpu.SemaphoreType.DMA((5,))],
        compiler_params=params(),
        name="pack",
    )(place, *(pltpu.with_memory_space_constraint(array, pltpu.HBM) for array in (query, key, value, taps, cotangent)))


def forward(blocks, chunks, recv, first_fwd, twist, second_fwd, second_inv, first_inv):
    first = blocks * chunks
    count = (4 * chunks + 1) * first
    return pl.pallas_call(
        lambda *refs: forward_kernel(blocks, chunks, *refs),
        out_shape=(
            jax.ShapeDtypeStruct((count, 2 * LANES), jnp.float32),
            jax.ShapeDtypeStruct((first, LANES), jnp.float32),
        ),
        in_specs=whole(6),
        out_specs=tuple(whole(2)),
        scratch_shapes=[pltpu.VMEM((count, 2 * LANES), jnp.bfloat16)] * 2,
        compiler_params=params(),
        name="forward",
    )(recv, first_fwd, twist, second_fwd, second_inv, first_inv)


def inverse(blocks, chunks, spec, twist, second_inv, first_inv):
    count = 4 * chunks * blocks * chunks
    return pl.pallas_call(
        lambda *refs: inverse_kernel(blocks, chunks, *refs),
        out_shape=jax.ShapeDtypeStruct((LANES * 2 * chunks, LANES), jnp.float32),
        in_specs=whole(4),
        out_specs=whole(1)[0],
        scratch_shapes=[pltpu.VMEM((count, 2 * LANES), jnp.bfloat16)] * 2,
        compiler_params=params(),
        cost_estimate=pl.CostEstimate(flops=10**9, bytes_accessed=4 * 10**6, transcendentals=0),
        name="inverse",
    )(spec, twist, second_inv, first_inv)


def fill(blocks, chunks, send, *terms):
    return pl.pallas_call(
        lambda *refs: fill_kernel(blocks, chunks, len(terms), *refs),
        out_shape=jax.ShapeDtypeStruct((LANES * 3 * chunks, LANES), jnp.float32),
        in_specs=whole(1 + len(terms)),
        out_specs=whole(1)[0],
        compiler_params=params(),
        name="fill",
    )(send, *terms)


def outputs(scale, recv, query, key, value, cotangent):
    length = query.shape[0]
    chunks = length // LANES
    rows = jax.ShapeDtypeStruct((length, LANES), jnp.bfloat16)
    return pl.pallas_call(
        lambda *refs: output_kernel(chunks, scale, *refs),
        out_shape=(rows, rows, rows, rows, jax.ShapeDtypeStruct((length, LANES), jnp.float32)),
        in_specs=whole(5),
        out_specs=tuple(whole(5)),
        compiler_params=params(),
        name="outputs",
    )(recv, query, key, value, cotangent)


def exchange(rows):
    shape = rows.shape
    flat = rows.reshape(LANES, 1, -1)
    return lax.all_to_all(flat, GROUP, 0, 0, tiled=True).reshape(shape)


def on_device(query, key, value, taps, cotangent):
    blocks = lax.axis_size("ctx")
    length = query.shape[0]
    chunks = length // LANES
    first_fwd, twist, second_fwd, second_inv, first_inv = (
        jnp.asarray(table) for table in dft_tables(blocks, chunks)
    )
    place = lax.axis_index(("y", "core")).astype(jnp.int32).reshape(1)
    recv = exchange(pack(place, query, key, value, taps, cotangent))
    spec, terms = forward(blocks, chunks, recv, first_fwd, twist, second_fwd, second_inv, first_inv)
    send = inverse(blocks, chunks, spec, twist, second_inv, first_inv)
    terms = terms + lax.ppermute(terms, "zh", PAIRS_NEAR)
    send = fill(blocks, chunks, send, terms, lax.ppermute(terms, "zh", PAIRS_ROUND))
    back = exchange(send)
    scale = 1.0 / math.sqrt(float(blocks * length * lax.axis_size(("y", "zh", "core"))))
    return outputs(scale, back, query, key, value, cotangent)


def solution(mesh):
    split_mesh = Mesh(mesh.devices.reshape(mesh.shape["ctx"], 4, 4, 2), ("ctx", "y", "zh", "core"))
    tp = ("y", "zh", "core")
    wide = P("ctx", tp)
    return jax.shard_map(
        on_device,
        mesh=split_mesh,
        in_specs=(wide, wide, wide, P("ctx", None), wide),
        out_specs=(wide, wide, wide, wide, P("ctx", None)),
        check_vma=False,
    )
```

```python
import math

import numpy as np
import ml_dtypes
import jax
import jax.numpy as jnp
from jax import lax
from jax.experimental import pallas as pl
from jax.experimental.pallas import tpu as pltpu
from jax.sharding import Mesh, PartitionSpec as P

LANES = 128
GROUP = ("ctx", "y", "core")
PAIRS_NEAR = [(0, 1), (1, 0), (2, 3), (3, 2)]
PAIRS_ROUND = [(0, 3), (3, 0), (1, 2), (2, 1)]


def split_const(table):
    high = table.astype(ml_dtypes.bfloat16)
    low = (table - high.astype(np.float64)).astype(ml_dtypes.bfloat16)
    return high, low


def dft_tables(blocks, chunks):
    first = blocks * chunks
    full = first * LANES
    order = (np.arange(blocks)[None, :] * chunks + np.arange(chunks)[:, None]).reshape(-1)
    k1 = np.arange(first)
    n2 = np.arange(LANES)
    angle = -2 * np.pi * (k1[:, None] * order[None, :] % first) / first + np.pi * order[None, :] / (2 * first)
    first_fwd = np.concatenate([np.cos(angle), np.sin(angle)], 0)
    high, low = split_const(first_fwd)
    first_fwd = np.concatenate([high, high, low], 1)
    high, low = split_const(np.concatenate([np.cos(angle).T, np.sin(angle).T], 1) / full)
    first_inv = np.concatenate([high, high, low], 1)
    angle = -2 * np.pi * (k1[:, None] * n2[None, :]) / full + np.pi * n2[None, :] / (2 * full)
    twist = np.concatenate([np.cos(angle), np.sin(angle)], 1).astype(np.float32)
    angle = 2 * np.pi * (n2[:, None] * n2[None, :] % LANES) / LANES
    cosine, sine = np.cos(angle), np.sin(angle)
    second = np.block([[cosine, -sine], [sine, cosine]])
    second_fwd = np.concatenate(split_const(second), 0)
    second_inv = np.concatenate(split_const(second.T), 0)
    return first_fwd, twist, second_fwd, second_inv, first_inv


def split(values):
    high = values.astype(jnp.bfloat16)
    return high, (values - high.astype(jnp.float32)).astype(jnp.bfloat16)


def dot(left, right):
    return jnp.dot(left, right, preferred_element_type=jnp.float32)


def second_stage(high, low, table):
    table_high = table[: 2 * LANES, :]
    table_low = table[2 * LANES :, :]
    return dot(high, table_high) + dot(low, table_high) + dot(high, table_low)


def pack_kernel(
    chunks, place_ref, query_hbm, key_hbm, value_hbm, taps_hbm, cotangent_hbm, send_ref,
    query_ref, key_ref, value_ref, taps_ref, cotangent_ref, done_ref,
):
    rows = 2 * chunks + 1
    place = place_ref[0]
    start = pl.multiple_of(lax.div(place, 2) * LANES, LANES)
    pairs = (
        (key_hbm, key_ref),
        (value_hbm, value_ref),
        (query_hbm, query_ref),
        (cotangent_hbm, cotangent_ref),
        (taps_hbm.at[pl.ds(start, LANES), :], taps_ref),
    )
    copies = [pltpu.make_async_copy(source, target, done_ref.at[n]) for n, (source, target) in enumerate(pairs)]
    for copy in copies:
        copy.start()
    copies[0].wait()
    copies[1].wait()
    for chunk in range(chunks):
        part = pl.ds(chunk * LANES, LANES)
        gate = key_ref[part, :].astype(jnp.float32) * value_ref[part, :].astype(jnp.float32)
        send_ref[pl.ds(chunk, LANES, stride=rows), :] = gate.T
    copies[2].wait()
    copies[3].wait()
    for chunk in range(chunks):
        part = pl.ds(chunk * LANES, LANES)
        grad = query_ref[part, :].astype(jnp.float32) * cotangent_ref[part, :].astype(jnp.float32)
        send_ref[pl.ds(chunks + chunk, LANES, stride=rows), :] = grad.T
    copies[4].wait()
    lane = lax.broadcasted_iota(jnp.int32, (LANES, LANES), 1)
    mine = lax.div(lane, LANES // 2) == lax.rem(place, 2)
    send_ref[pl.ds(2 * chunks, LANES, stride=rows), :] = jnp.where(mine, taps_ref[...].T, 0.0)


def forward_kernel(
    blocks, chunks, recv_ref, first_ref, twist_ref, second_ref, inverse_ref, first_inv_ref, spec_ref, terms_ref, high_ref, low_ref
):
    rows = 2 * chunks + 1
    first = blocks * chunks
    columns = 2 * chunks
    stride = columns * rows
    cosine = twist_ref[:, :LANES]
    sine = twist_ref[:, LANES:]

    def read(column, signal):
        return jnp.concatenate(
            [recv_ref[pl.ds(column * rows + signal * chunks + chunk, blocks, stride=stride), :] for chunk in range(chunks)], 0
        )

    taps = jnp.concatenate(
        [
            recv_ref[pl.ds(2 * chunk * rows + rows - 1, blocks, stride=stride), :]
            + recv_ref[pl.ds((2 * chunk + 1) * rows + rows - 1, blocks, stride=stride), :]
            for chunk in range(chunks)
        ],
        0,
    )
    signals = [read(column, signal) for signal in range(2) for column in range(columns)] + [taps]
    for start in range(0, len(signals), 2):
        group = signals[start : start + 2]
        wide = jnp.concatenate(group, 1) if len(group) > 1 else group[0]
        high, low = split(wide)
        mixed = dot(first_ref[...], jnp.concatenate([high, low, high], 0))
        for offset in range(len(group)):
            lanes = slice(offset * LANES, (offset + 1) * LANES)
            real, imag = mixed[:first, lanes], mixed[first:, lanes]
            high, low = split(jnp.concatenate([real * cosine - imag * sine, imag * cosine + real * sine], 1))
            place = pl.ds((start + offset) * first, first)
            high_ref[place, :] = high
            low_ref[place, :] = low
    spec_ref[...] = second_stage(high_ref[...], low_ref[...], second_ref)
    real = jnp.zeros((first, LANES), jnp.float32)
    imag = jnp.zeros((first, LANES), jnp.float32)
    for column in range(columns):
        gate = pl.ds(column * first, first)
        grad = pl.ds((columns + column) * first, first)
        gate_real, gate_imag = spec_ref[gate, :LANES], spec_ref[gate, LANES:]
        grad_real, grad_imag = spec_ref[grad, :LANES], spec_ref[grad, LANES:]
        real = real + grad_real * gate_real + grad_imag * gate_imag
        imag = imag + grad_imag * gate_real - grad_real * gate_imag
    high, low = split(jnp.concatenate([real, imag], 1))
    back = second_stage(high, low, inverse_ref)
    real, imag = back[:, :LANES], back[:, LANES:]
    high, low = split(jnp.concatenate([real * cosine + imag * sine, imag * cosine - real * sine], 0))
    terms_ref[...] = dot(first_inv_ref[...], jnp.concatenate([high, low, high], 0))


def inverse_kernel(blocks, chunks, spec_ref, twist_ref, inverse_ref, first_inv_ref, send_ref, high_ref, low_ref):
    first = blocks * chunks
    columns = 2 * chunks
    cosine = twist_ref[:, :LANES]
    sine = twist_ref[:, LANES:]
    taps = pl.ds(2 * columns * first, first)
    taps_real, taps_imag = spec_ref[taps, :LANES], spec_ref[taps, LANES:]
    for column in range(columns):
        place = pl.ds(column * first, first)
        real, imag = spec_ref[place, :LANES], spec_ref[place, LANES:]
        high, low = split(jnp.concatenate([real * taps_real - imag * taps_imag, real * taps_imag + imag * taps_real], 1))
        high_ref[place, :] = high
        low_ref[place, :] = low
        place = pl.ds((columns + column) * first, first)
        real, imag = spec_ref[place, :LANES], spec_ref[place, LANES:]
        high, low = split(jnp.concatenate([real * taps_real + imag * taps_imag, imag * taps_real - real * taps_imag], 1))
        high_ref[place, :] = high
        low_ref[place, :] = low
    rows = 2 * chunks
    stride = columns * rows
    back = second_stage(high_ref[...], low_ref[...], inverse_ref)
    for signal in range(2):
        for column in range(0, columns, 2):
            sides = []
            for offset in range(2):
                begin = (signal * columns + column + offset) * first
                real, imag = back[begin : begin + first, :LANES], back[begin : begin + first, LANES:]
                sides.append(jnp.concatenate([real * cosine + imag * sine, imag * cosine - real * sine], 0))
            high, low = split(jnp.concatenate(sides, 1))
            result = dot(first_inv_ref[...], jnp.concatenate([high, low, high], 0))
            for offset in range(2):
                for chunk in range(chunks):
                    send_ref[pl.ds((column + offset) * rows + signal * chunks + chunk, blocks, stride=stride), :] = result[
                        chunk * blocks : (chunk + 1) * blocks, offset * LANES : (offset + 1) * LANES
                    ]


def fill_kernel(blocks, chunks, count, conv_ref, *refs):
    columns = 2 * chunks
    rows = 3 * chunks
    total = refs[0][...]
    for ref in refs[1:count]:
        total = total + ref[...]
    send_ref = refs[count]
    for place in range(blocks * columns):
        send_ref[pl.ds(place * rows, 2 * chunks), :] = conv_ref[pl.ds(place * 2 * chunks, 2 * chunks), :]
    for chunk in range(chunks):
        piece = total[chunk * blocks : (chunk + 1) * blocks, :]
        for column in range(columns):
            send_ref[pl.ds(column * rows + 2 * chunks + chunk, blocks, stride=columns * rows), :] = piece


def output_kernel(
    chunks, scale, recv_ref, query_ref, key_ref, value_ref, cotangent_ref,
    gated_ref, grad_query_ref, grad_key_ref, grad_value_ref, grad_taps_ref,
):
    rows = 3 * chunks
    for chunk in range(chunks):
        part = pl.ds(chunk * LANES, LANES)
        conv = recv_ref[pl.ds(chunk, LANES, stride=rows), :].T
        gated_ref[part, :] = (query_ref[part, :].astype(jnp.float32) * conv).astype(jnp.bfloat16)
        grad_query_ref[part, :] = (cotangent_ref[part, :].astype(jnp.float32) * conv).astype(jnp.bfloat16)
        grad_gate = recv_ref[pl.ds(chunks + chunk, LANES, stride=rows), :].T
        grad_key_ref[part, :] = (grad_gate * value_ref[part, :].astype(jnp.float32)).astype(jnp.bfloat16)
        grad_value_ref[part, :] = (grad_gate * key_ref[part, :].astype(jnp.float32)).astype(jnp.bfloat16)
        grad_taps_ref[part, :] = recv_ref[pl.ds(2 * chunks + chunk, LANES, stride=rows), :].T * scale


def params():
    return pltpu.CompilerParams(vmem_limit_bytes=48 * 1024 * 1024)


def whole(count):
    return [pl.BlockSpec(memory_space=pltpu.VMEM)] * count


def pack(place, query, key, value, taps, cotangent):
    length = query.shape[0]
    chunks = length // LANES
    wide = pltpu.VMEM((length, LANES), jnp.bfloat16)
    return pl.pallas_call(
        lambda *refs: pack_kernel(chunks, *refs),
        out_shape=jax.ShapeDtypeStruct((LANES * (2 * chunks + 1), LANES), jnp.float32),
        in_specs=[pl.BlockSpec(memory_space=pltpu.SMEM)] + [pl.BlockSpec(memory_space=pltpu.HBM)] * 5,
        out_specs=whole(1)[0],
        scratch_shapes=[wide, wide, wide, pltpu.VMEM((LANES, LANES), jnp.float32), wide, pltpu.SemaphoreType.DMA((5,))],
        compiler_params=params(),
        name="pack",
    )(place, *(pltpu.with_memory_space_constraint(array, pltpu.HBM) for array in (query, key, value, taps, cotangent)))


def forward(blocks, chunks, recv, first_fwd, twist, second_fwd, second_inv, first_inv):
    first = blocks * chunks
    count = (4 * chunks + 1) * first
    return pl.pallas_call(
        lambda *refs: forward_kernel(blocks, chunks, *refs),
        out_shape=(
            jax.ShapeDtypeStruct((count, 2 * LANES), jnp.float32),
            jax.ShapeDtypeStruct((first, LANES), jnp.float32),
        ),
        in_specs=whole(6),
        out_specs=tuple(whole(2)),
        scratch_shapes=[pltpu.VMEM((count, 2 * LANES), jnp.bfloat16)] * 2,
        compiler_params=params(),
        name="forward",
    )(recv, first_fwd, twist, second_fwd, second_inv, first_inv)


def inverse(blocks, chunks, spec, twist, second_inv, first_inv):
    count = 4 * chunks * blocks * chunks
    return pl.pallas_call(
        lambda *refs: inverse_kernel(blocks, chunks, *refs),
        out_shape=jax.ShapeDtypeStruct((LANES * 2 * chunks, LANES), jnp.float32),
        in_specs=whole(4),
        out_specs=whole(1)[0],
        scratch_shapes=[pltpu.VMEM((count, 2 * LANES), jnp.bfloat16)] * 2,
        compiler_params=params(),
        cost_estimate=pl.CostEstimate(flops=10**9, bytes_accessed=4 * 10**6, transcendentals=0),
        name="inverse",
    )(spec, twist, second_inv, first_inv)


def fill(blocks, chunks, send, *terms):
    return pl.pallas_call(
        lambda *refs: fill_kernel(blocks, chunks, len(terms), *refs),
        out_shape=jax.ShapeDtypeStruct((LANES * 3 * chunks, LANES), jnp.float32),
        in_specs=whole(1 + len(terms)),
        out_specs=whole(1)[0],
        compiler_params=params(),
        name="fill",
    )(send, *terms)


def outputs(scale, recv, query, key, value, cotangent):
    length = query.shape[0]
    chunks = length // LANES
    rows = jax.ShapeDtypeStruct((length, LANES), jnp.bfloat16)
    return pl.pallas_call(
        lambda *refs: output_kernel(chunks, scale, *refs),
        out_shape=(rows, rows, rows, rows, jax.ShapeDtypeStruct((length, LANES), jnp.float32)),
        in_specs=whole(5),
        out_specs=tuple(whole(5)),
        compiler_params=params(),
        name="outputs",
    )(recv, query, key, value, cotangent)


def by_core(*pairs):
    return [(2 * a + core, 2 * b + core) for core in range(2) for a, b in pairs[core]]


def exchange(rows):
    shape = rows.shape
    flat = rows.reshape(LANES, 1, -1)
    return lax.all_to_all(flat, GROUP, 0, 0, tiled=True).reshape(shape)


def on_device(query, key, value, taps, cotangent):
    blocks = lax.axis_size("ctx")
    length = query.shape[0]
    chunks = length // LANES
    first_fwd, twist, second_fwd, second_inv, first_inv = (
        jnp.asarray(table) for table in dft_tables(blocks, chunks)
    )
    place = lax.axis_index(("y", "core")).astype(jnp.int32).reshape(1)
    recv = exchange(pack(place, query, key, value, taps, cotangent))
    spec, terms = forward(blocks, chunks, recv, first_fwd, twist, second_fwd, second_inv, first_inv)
    send = inverse(blocks, chunks, spec, twist, second_inv, first_inv)
    terms = terms + lax.ppermute(terms, ("zh", "core"), by_core(PAIRS_NEAR, PAIRS_ROUND))
    send = fill(blocks, chunks, send, terms, lax.ppermute(terms, ("zh", "core"), by_core(PAIRS_ROUND, PAIRS_NEAR)))
    back = exchange(send)
    scale = 1.0 / math.sqrt(float(blocks * length * lax.axis_size(("y", "zh", "core"))))
    return outputs(scale, back, query, key, value, cotangent)


def solution(mesh):
    split_mesh = Mesh(mesh.devices.reshape(mesh.shape["ctx"], 4, 4, 2), ("ctx", "y", "zh", "core"))
    tp = ("y", "zh", "core")
    wide = P("ctx", tp)
    return jax.shard_map(
        on_device,
        mesh=split_mesh,
        in_specs=(wide, wide, wide, P("ctx", None), wide),
        out_specs=(wide, wide, wide, wide, P("ctx", None)),
        check_vma=False,
    )
```

```python
import math

import numpy as np
import ml_dtypes
import jax
import jax.numpy as jnp
from jax import lax
from jax.experimental import pallas as pl
from jax.experimental.pallas import tpu as pltpu
from jax.sharding import Mesh, PartitionSpec as P

LANES = 128
GROUP = ("ctx", "y", "core")
PAIRS_NEAR = [(0, 1), (1, 0), (2, 3), (3, 2)]
PAIRS_ROUND = [(0, 3), (3, 0), (1, 2), (2, 1)]


def split_const(table):
    high = table.astype(ml_dtypes.bfloat16)
    low = (table - high.astype(np.float64)).astype(ml_dtypes.bfloat16)
    return high, low


def dft_tables(blocks, chunks):
    first = blocks * chunks
    full = first * LANES
    order = (np.arange(blocks)[None, :] * chunks + np.arange(chunks)[:, None]).reshape(-1)
    k1 = np.arange(first)
    n2 = np.arange(LANES)
    angle = -2 * np.pi * (k1[:, None] * order[None, :] % first) / first + np.pi * order[None, :] / (2 * first)
    first_fwd = np.concatenate([np.cos(angle), np.sin(angle)], 0)
    high, low = split_const(first_fwd)
    first_fwd = np.concatenate([high, high, low], 1)
    high, low = split_const(np.concatenate([np.cos(angle).T, np.sin(angle).T], 1) / full)
    first_inv = np.concatenate([high, high, low], 1)
    angle = -2 * np.pi * (k1[:, None] * n2[None, :]) / full + np.pi * n2[None, :] / (2 * full)
    twist = np.concatenate([np.cos(angle), np.sin(angle)], 1).astype(np.float32)
    angle = 2 * np.pi * (n2[:, None] * n2[None, :] % LANES) / LANES
    cosine, sine = np.cos(angle), np.sin(angle)
    second = np.block([[cosine, -sine], [sine, cosine]])
    second_fwd = np.concatenate(split_const(second), 0)
    second_inv = np.concatenate(split_const(second.T), 0)
    return first_fwd, twist, second_fwd, second_inv, first_inv


def split(values):
    high = values.astype(jnp.bfloat16)
    return high, (values - high.astype(jnp.float32)).astype(jnp.bfloat16)


def dot(left, right):
    return jnp.dot(left, right, preferred_element_type=jnp.float32)


def second_stage(high, low, table):
    table_high = table[: 2 * LANES, :]
    table_low = table[2 * LANES :, :]
    return dot(high, table_high) + dot(low, table_high) + dot(high, table_low)


def pack_kernel(
    chunks, place_ref, query_hbm, key_hbm, value_hbm, taps_hbm, cotangent_hbm, send_ref,
    query_ref, key_ref, value_ref, taps_ref, cotangent_ref, done_ref,
):
    rows = 2 * chunks + 1
    place = place_ref[0]
    start = pl.multiple_of(lax.div(place, 2) * LANES, LANES)
    pairs = (
        (key_hbm, key_ref),
        (value_hbm, value_ref),
        (query_hbm, query_ref),
        (cotangent_hbm, cotangent_ref),
        (taps_hbm.at[pl.ds(start, LANES), :], taps_ref),
    )
    copies = [pltpu.make_async_copy(source, target, done_ref.at[n]) for n, (source, target) in enumerate(pairs)]
    for copy in copies:
        copy.start()
    copies[0].wait()
    copies[1].wait()
    for chunk in range(chunks):
        part = pl.ds(chunk * LANES, LANES)
        gate = key_ref[part, :].astype(jnp.float32) * value_ref[part, :].astype(jnp.float32)
        send_ref[pl.ds(chunk, LANES, stride=rows), :] = gate.T
    copies[2].wait()
    copies[3].wait()
    for chunk in range(chunks):
        part = pl.ds(chunk * LANES, LANES)
        grad = query_ref[part, :].astype(jnp.float32) * cotangent_ref[part, :].astype(jnp.float32)
        send_ref[pl.ds(chunks + chunk, LANES, stride=rows), :] = grad.T
    copies[4].wait()
    lane = lax.broadcasted_iota(jnp.int32, (LANES, LANES), 1)
    mine = lax.div(lane, LANES // 2) == lax.rem(place, 2)
    send_ref[pl.ds(2 * chunks, LANES, stride=rows), :] = jnp.where(mine, taps_ref[...].T, 0.0)


def forward_kernel(
    blocks, chunks, recv_ref, first_ref, twist_ref, second_ref, inverse_ref, first_inv_ref, spec_ref, terms_ref, high_ref, low_ref
):
    rows = 2 * chunks + 1
    first = blocks * chunks
    columns = 2 * chunks
    stride = columns * rows
    cosine = twist_ref[:, :LANES]
    sine = twist_ref[:, LANES:]

    def read(column, signal):
        return jnp.concatenate(
            [recv_ref[pl.ds(column * rows + signal * chunks + chunk, blocks, stride=stride), :] for chunk in range(chunks)], 0
        )

    taps = jnp.concatenate(
        [
            recv_ref[pl.ds(2 * chunk * rows + rows - 1, blocks, stride=stride), :]
            + recv_ref[pl.ds((2 * chunk + 1) * rows + rows - 1, blocks, stride=stride), :]
            for chunk in range(chunks)
        ],
        0,
    )
    signals = [read(column, signal) for signal in range(2) for column in range(columns)] + [taps]
    for start in range(0, len(signals), 2):
        group = signals[start : start + 2]
        wide = jnp.concatenate(group, 1) if len(group) > 1 else group[0]
        high, low = split(wide)
        mixed = dot(first_ref[...], jnp.concatenate([high, low, high], 0))
        for offset in range(len(group)):
            lanes = slice(offset * LANES, (offset + 1) * LANES)
            real, imag = mixed[:first, lanes], mixed[first:, lanes]
            high, low = split(jnp.concatenate([real * cosine - imag * sine, imag * cosine + real * sine], 1))
            place = pl.ds((start + offset) * first, first)
            high_ref[place, :] = high
            low_ref[place, :] = low
        if (start + len(group)) % columns == 0 or len(group) == 1:
            begin = start + len(group) - (columns if len(group) > 1 else 1)
            done = pl.ds(begin * first, (start + len(group) - begin) * first)
            spec_ref[done, :] = second_stage(high_ref[done, :], low_ref[done, :], second_ref)
    real = jnp.zeros((first, LANES), jnp.float32)
    imag = jnp.zeros((first, LANES), jnp.float32)
    for column in range(columns):
        gate = pl.ds(column * first, first)
        grad = pl.ds((columns + column) * first, first)
        gate_real, gate_imag = spec_ref[gate, :LANES], spec_ref[gate, LANES:]
        grad_real, grad_imag = spec_ref[grad, :LANES], spec_ref[grad, LANES:]
        real = real + grad_real * gate_real + grad_imag * gate_imag
        imag = imag + grad_imag * gate_real - grad_real * gate_imag
    high, low = split(jnp.concatenate([real, imag], 1))
    back = second_stage(high, low, inverse_ref)
    real, imag = back[:, :LANES], back[:, LANES:]
    high, low = split(jnp.concatenate([real * cosine + imag * sine, imag * cosine - real * sine], 0))
    terms_ref[...] = dot(first_inv_ref[...], jnp.concatenate([high, low, high], 0))


def inverse_kernel(blocks, chunks, spec_ref, twist_ref, inverse_ref, first_inv_ref, send_ref, high_ref, low_ref):
    first = blocks * chunks
    columns = 2 * chunks
    cosine = twist_ref[:, :LANES]
    sine = twist_ref[:, LANES:]
    taps = pl.ds(2 * columns * first, first)
    taps_real, taps_imag = spec_ref[taps, :LANES], spec_ref[taps, LANES:]
    for column in range(columns):
        place = pl.ds(column * first, first)
        real, imag = spec_ref[place, :LANES], spec_ref[place, LANES:]
        high, low = split(jnp.concatenate([real * taps_real - imag * taps_imag, real * taps_imag + imag * taps_real], 1))
        high_ref[place, :] = high
        low_ref[place, :] = low
        place = pl.ds((columns + column) * first, first)
        real, imag = spec_ref[place, :LANES], spec_ref[place, LANES:]
        high, low = split(jnp.concatenate([real * taps_real + imag * taps_imag, imag * taps_real - real * taps_imag], 1))
        high_ref[place, :] = high
        low_ref[place, :] = low
    rows = 2 * chunks
    stride = columns * rows
    back = second_stage(high_ref[...], low_ref[...], inverse_ref)
    for signal in range(2):
        for column in range(0, columns, 2):
            sides = []
            for offset in range(2):
                begin = (signal * columns + column + offset) * first
                real, imag = back[begin : begin + first, :LANES], back[begin : begin + first, LANES:]
                sides.append(jnp.concatenate([real * cosine + imag * sine, imag * cosine - real * sine], 0))
            high, low = split(jnp.concatenate(sides, 1))
            result = dot(first_inv_ref[...], jnp.concatenate([high, low, high], 0))
            for offset in range(2):
                for chunk in range(chunks):
                    send_ref[pl.ds((column + offset) * rows + signal * chunks + chunk, blocks, stride=stride), :] = result[
                        chunk * blocks : (chunk + 1) * blocks, offset * LANES : (offset + 1) * LANES
                    ]


def fill_kernel(blocks, chunks, count, conv_ref, *refs):
    columns = 2 * chunks
    rows = 3 * chunks
    total = refs[0][...]
    for ref in refs[1:count]:
        total = total + ref[...]
    send_ref = refs[count]
    for place in range(blocks * columns):
        send_ref[pl.ds(place * rows, 2 * chunks), :] = conv_ref[pl.ds(place * 2 * chunks, 2 * chunks), :]
    for chunk in range(chunks):
        piece = total[chunk * blocks : (chunk + 1) * blocks, :]
        for column in range(columns):
            send_ref[pl.ds(column * rows + 2 * chunks + chunk, blocks, stride=columns * rows), :] = piece


def output_kernel(
    chunks, scale, recv_ref, query_ref, key_ref, value_ref, cotangent_ref,
    gated_ref, grad_query_ref, grad_key_ref, grad_value_ref, grad_taps_ref,
):
    rows = 3 * chunks
    for chunk in range(chunks):
        part = pl.ds(chunk * LANES, LANES)
        conv = recv_ref[pl.ds(chunk, LANES, stride=rows), :].T
        gated_ref[part, :] = (query_ref[part, :].astype(jnp.float32) * conv).astype(jnp.bfloat16)
        grad_query_ref[part, :] = (cotangent_ref[part, :].astype(jnp.float32) * conv).astype(jnp.bfloat16)
        grad_gate = recv_ref[pl.ds(chunks + chunk, LANES, stride=rows), :].T
        grad_key_ref[part, :] = (grad_gate * value_ref[part, :].astype(jnp.float32)).astype(jnp.bfloat16)
        grad_value_ref[part, :] = (grad_gate * key_ref[part, :].astype(jnp.float32)).astype(jnp.bfloat16)
        grad_taps_ref[part, :] = recv_ref[pl.ds(2 * chunks + chunk, LANES, stride=rows), :].T * scale


def params():
    return pltpu.CompilerParams(vmem_limit_bytes=48 * 1024 * 1024)


def whole(count):
    return [pl.BlockSpec(memory_space=pltpu.VMEM)] * count


def pack(place, query, key, value, taps, cotangent):
    length = query.shape[0]
    chunks = length // LANES
    wide = pltpu.VMEM((length, LANES), jnp.bfloat16)
    return pl.pallas_call(
        lambda *refs: pack_kernel(chunks, *refs),
        out_shape=jax.ShapeDtypeStruct((LANES * (2 * chunks + 1), LANES), jnp.float32),
        in_specs=[pl.BlockSpec(memory_space=pltpu.SMEM)] + [pl.BlockSpec(memory_space=pltpu.HBM)] * 5,
        out_specs=whole(1)[0],
        scratch_shapes=[wide, wide, wide, pltpu.VMEM((LANES, LANES), jnp.float32), wide, pltpu.SemaphoreType.DMA((5,))],
        compiler_params=params(),
        name="pack",
    )(place, *(pltpu.with_memory_space_constraint(array, pltpu.HBM) for array in (query, key, value, taps, cotangent)))


def forward(blocks, chunks, recv, first_fwd, twist, second_fwd, second_inv, first_inv):
    first = blocks * chunks
    count = (4 * chunks + 1) * first
    return pl.pallas_call(
        lambda *refs: forward_kernel(blocks, chunks, *refs),
        out_shape=(
            jax.ShapeDtypeStruct((count, 2 * LANES), jnp.float32),
            jax.ShapeDtypeStruct((first, LANES), jnp.float32),
        ),
        in_specs=whole(6),
        out_specs=tuple(whole(2)),
        scratch_shapes=[pltpu.VMEM((count, 2 * LANES), jnp.bfloat16)] * 2,
        compiler_params=params(),
        name="forward",
    )(recv, first_fwd, twist, second_fwd, second_inv, first_inv)


def inverse(blocks, chunks, spec, twist, second_inv, first_inv):
    count = 4 * chunks * blocks * chunks
    return pl.pallas_call(
        lambda *refs: inverse_kernel(blocks, chunks, *refs),
        out_shape=jax.ShapeDtypeStruct((LANES * 2 * chunks, LANES), jnp.float32),
        in_specs=whole(4),
        out_specs=whole(1)[0],
        scratch_shapes=[pltpu.VMEM((count, 2 * LANES), jnp.bfloat16)] * 2,
        compiler_params=params(),
        cost_estimate=pl.CostEstimate(flops=10**9, bytes_accessed=4 * 10**6, transcendentals=0),
        name="inverse",
    )(spec, twist, second_inv, first_inv)


def fill(blocks, chunks, send, *terms):
    return pl.pallas_call(
        lambda *refs: fill_kernel(blocks, chunks, len(terms), *refs),
        out_shape=jax.ShapeDtypeStruct((LANES * 3 * chunks, LANES), jnp.float32),
        in_specs=whole(1 + len(terms)),
        out_specs=whole(1)[0],
        compiler_params=params(),
        name="fill",
    )(send, *terms)


def outputs(scale, recv, query, key, value, cotangent):
    length = query.shape[0]
    chunks = length // LANES
    rows = jax.ShapeDtypeStruct((length, LANES), jnp.bfloat16)
    return pl.pallas_call(
        lambda *refs: output_kernel(chunks, scale, *refs),
        out_shape=(rows, rows, rows, rows, jax.ShapeDtypeStruct((length, LANES), jnp.float32)),
        in_specs=whole(5),
        out_specs=tuple(whole(5)),
        compiler_params=params(),
        name="outputs",
    )(recv, query, key, value, cotangent)


def by_core(*pairs):
    return [(2 * a + core, 2 * b + core) for core in range(2) for a, b in pairs[core]]


def exchange(rows):
    shape = rows.shape
    flat = rows.reshape(LANES, 1, -1)
    return lax.all_to_all(flat, GROUP, 0, 0, tiled=True).reshape(shape)


def on_device(query, key, value, taps, cotangent):
    blocks = lax.axis_size("ctx")
    length = query.shape[0]
    chunks = length // LANES
    first_fwd, twist, second_fwd, second_inv, first_inv = (
        jnp.asarray(table) for table in dft_tables(blocks, chunks)
    )
    place = lax.axis_index(("y", "core")).astype(jnp.int32).reshape(1)
    recv = exchange(pack(place, query, key, value, taps, cotangent))
    spec, terms = forward(blocks, chunks, recv, first_fwd, twist, second_fwd, second_inv, first_inv)
    send = inverse(blocks, chunks, spec, twist, second_inv, first_inv)
    terms = terms + lax.ppermute(terms, ("zh", "core"), by_core(PAIRS_NEAR, PAIRS_ROUND))
    send = fill(blocks, chunks, send, terms, lax.ppermute(terms, ("zh", "core"), by_core(PAIRS_ROUND, PAIRS_NEAR)))
    back = exchange(send)
    scale = 1.0 / math.sqrt(float(blocks * length * lax.axis_size(("y", "zh", "core"))))
    return outputs(scale, back, query, key, value, cotangent)


def solution(mesh):
    split_mesh = Mesh(mesh.devices.reshape(mesh.shape["ctx"], 4, 4, 2), ("ctx", "y", "zh", "core"))
    tp = ("y", "zh", "core")
    wide = P("ctx", tp)
    return jax.shard_map(
        on_device,
        mesh=split_mesh,
        in_specs=(wide, wide, wide, P("ctx", None), wide),
        out_specs=(wide, wide, wide, wide, P("ctx", None)),
        check_vma=False,
    )
```

```python
import math

import numpy as np
import ml_dtypes
import jax
import jax.numpy as jnp
from jax import lax
from jax.experimental import pallas as pl
from jax.experimental.pallas import tpu as pltpu
from jax.sharding import Mesh, PartitionSpec as P

LANES = 128
GROUP = ("ctx", "y", "core")
PAIRS_NEAR = [(0, 1), (1, 0), (2, 3), (3, 2)]
PAIRS_ROUND = [(0, 3), (3, 0), (1, 2), (2, 1)]


def split_const(table):
    high = table.astype(ml_dtypes.bfloat16)
    low = (table - high.astype(np.float64)).astype(ml_dtypes.bfloat16)
    return high, low


def dft_tables(blocks, chunks):
    first = blocks * chunks
    full = first * LANES
    order = (np.arange(blocks)[None, :] * chunks + np.arange(chunks)[:, None]).reshape(-1)
    k1 = np.arange(first)
    n2 = np.arange(LANES)
    angle = -2 * np.pi * (k1[:, None] * order[None, :] % first) / first + np.pi * order[None, :] / (2 * first)
    first_fwd = np.concatenate([np.cos(angle), np.sin(angle)], 0)
    high, low = split_const(first_fwd)
    first_fwd = np.concatenate([high, high, low], 1)
    high, low = split_const(np.concatenate([np.cos(angle).T, np.sin(angle).T], 1) / full)
    first_inv = np.concatenate([high, high, low], 1)
    angle = -2 * np.pi * (k1[:, None] * n2[None, :]) / full + np.pi * n2[None, :] / (2 * full)
    twist = np.concatenate([np.cos(angle), np.sin(angle)], 1).astype(np.float32)
    angle = 2 * np.pi * (n2[:, None] * n2[None, :] % LANES) / LANES
    cosine, sine = np.cos(angle), np.sin(angle)
    second = np.block([[cosine, -sine], [sine, cosine]])
    second_fwd = np.concatenate(split_const(second), 0)
    second_inv = np.concatenate(split_const(second.T), 0)
    return first_fwd, twist, second_fwd, second_inv, first_inv


def split(values):
    high = values.astype(jnp.bfloat16)
    return high, (values - high.astype(jnp.float32)).astype(jnp.bfloat16)


def dot(left, right):
    return jnp.dot(left, right, preferred_element_type=jnp.float32)


def second_stage(high, low, table):
    table_high = table[: 2 * LANES, :]
    table_low = table[2 * LANES :, :]
    return dot(high, table_high) + dot(low, table_high) + dot(high, table_low)


def pack_kernel(
    chunks, place_ref, query_hbm, key_hbm, value_hbm, taps_hbm, cotangent_hbm, send_ref,
    query_ref, key_ref, value_ref, taps_ref, cotangent_ref, done_ref,
):
    rows = 2 * chunks + 1
    place = place_ref[0]
    start = pl.multiple_of(lax.div(place, 2) * LANES, LANES)
    pairs = (
        (key_hbm, key_ref),
        (value_hbm, value_ref),
        (query_hbm, query_ref),
        (cotangent_hbm, cotangent_ref),
        (taps_hbm.at[pl.ds(start, LANES), :], taps_ref),
    )
    copies = [pltpu.make_async_copy(source, target, done_ref.at[n]) for n, (source, target) in enumerate(pairs)]
    for copy in copies:
        copy.start()
    copies[0].wait()
    copies[1].wait()
    for chunk in range(chunks):
        part = pl.ds(chunk * LANES, LANES)
        gate = key_ref[part, :].astype(jnp.float32) * value_ref[part, :].astype(jnp.float32)
        send_ref[pl.ds(chunk, LANES, stride=rows), :] = gate.T
    copies[2].wait()
    copies[3].wait()
    for chunk in range(chunks):
        part = pl.ds(chunk * LANES, LANES)
        grad = query_ref[part, :].astype(jnp.float32) * cotangent_ref[part, :].astype(jnp.float32)
        send_ref[pl.ds(chunks + chunk, LANES, stride=rows), :] = grad.T
    copies[4].wait()
    lane = lax.broadcasted_iota(jnp.int32, (LANES, LANES), 1)
    mine = lax.div(lane, LANES // 2) == lax.rem(place, 2)
    send_ref[pl.ds(2 * chunks, LANES, stride=rows), :] = jnp.where(mine, taps_ref[...].T, 0.0)


def forward_kernel(
    blocks, chunks, recv_ref, first_ref, twist_ref, second_ref, inverse_ref, first_inv_ref, spec_ref, terms_ref, high_ref, low_ref
):
    rows = 2 * chunks + 1
    first = blocks * chunks
    columns = 2 * chunks
    stride = columns * rows
    cosine = twist_ref[:, :LANES]
    sine = twist_ref[:, LANES:]

    def read(column, signal):
        return jnp.concatenate(
            [recv_ref[pl.ds(column * rows + signal * chunks + chunk, blocks, stride=stride), :] for chunk in range(chunks)], 0
        )

    signals = [read(column, signal) for signal in range(2) for column in range(columns)]
    for start in range(0, len(signals), 2):
        group = signals[start : start + 2]
        high, low = split(jnp.concatenate(group, 1))
        mixed = dot(first_ref[...], jnp.concatenate([high, low, high], 0))
        for offset in range(len(group)):
            lanes = slice(offset * LANES, (offset + 1) * LANES)
            real, imag = mixed[:first, lanes], mixed[first:, lanes]
            high, low = split(jnp.concatenate([real * cosine - imag * sine, imag * cosine + real * sine], 1))
            place = pl.ds((start + offset) * first, first)
            high_ref[place, :] = high
            low_ref[place, :] = low
        if (start + len(group)) % columns == 0:
            done = pl.ds((start + len(group) - columns) * first, columns * first)
            spec_ref[done, :] = second_stage(high_ref[done, :], low_ref[done, :], second_ref)
    real = jnp.zeros((first, LANES), jnp.float32)
    imag = jnp.zeros((first, LANES), jnp.float32)
    for column in range(columns):
        gate = pl.ds(column * first, first)
        grad = pl.ds((columns + column) * first, first)
        gate_real, gate_imag = spec_ref[gate, :LANES], spec_ref[gate, LANES:]
        grad_real, grad_imag = spec_ref[grad, :LANES], spec_ref[grad, LANES:]
        real = real + grad_real * gate_real + grad_imag * gate_imag
        imag = imag + grad_imag * gate_real - grad_real * gate_imag
    high, low = split(jnp.concatenate([real, imag], 1))
    back = second_stage(high, low, inverse_ref)
    real, imag = back[:, :LANES], back[:, LANES:]
    high, low = split(jnp.concatenate([real * cosine + imag * sine, imag * cosine - real * sine], 0))
    terms_ref[...] = dot(first_inv_ref[...], jnp.concatenate([high, low, high], 0))


def inverse_kernel(
    blocks, chunks, recv_ref, spec_ref, first_ref, twist_ref, second_ref, inverse_ref, first_inv_ref, send_ref, high_ref, low_ref
):
    first = blocks * chunks
    columns = 2 * chunks
    cosine = twist_ref[:, :LANES]
    sine = twist_ref[:, LANES:]
    rows = 2 * chunks + 1
    stride = columns * rows
    taps = jnp.concatenate(
        [
            recv_ref[pl.ds(2 * chunk * rows + rows - 1, blocks, stride=stride), :]
            + recv_ref[pl.ds((2 * chunk + 1) * rows + rows - 1, blocks, stride=stride), :]
            for chunk in range(chunks)
        ],
        0,
    )
    high, low = split(taps)
    mixed = dot(first_ref[...], jnp.concatenate([high, low, high], 0))
    real, imag = mixed[:first, :], mixed[first:, :]
    high, low = split(jnp.concatenate([real * cosine - imag * sine, imag * cosine + real * sine], 1))
    taps_spec = second_stage(high, low, second_ref)
    taps_real, taps_imag = taps_spec[:, :LANES], taps_spec[:, LANES:]
    for column in range(columns):
        place = pl.ds(column * first, first)
        real, imag = spec_ref[place, :LANES], spec_ref[place, LANES:]
        high, low = split(jnp.concatenate([real * taps_real - imag * taps_imag, real * taps_imag + imag * taps_real], 1))
        high_ref[place, :] = high
        low_ref[place, :] = low
        place = pl.ds((columns + column) * first, first)
        real, imag = spec_ref[place, :LANES], spec_ref[place, LANES:]
        high, low = split(jnp.concatenate([real * taps_real + imag * taps_imag, imag * taps_real - real * taps_imag], 1))
        high_ref[place, :] = high
        low_ref[place, :] = low
    rows = 2 * chunks
    stride = columns * rows
    back = second_stage(high_ref[...], low_ref[...], inverse_ref)
    for signal in range(2):
        for column in range(0, columns, 2):
            sides = []
            for offset in range(2):
                begin = (signal * columns + column + offset) * first
                real, imag = back[begin : begin + first, :LANES], back[begin : begin + first, LANES:]
                sides.append(jnp.concatenate([real * cosine + imag * sine, imag * cosine - real * sine], 0))
            high, low = split(jnp.concatenate(sides, 1))
            result = dot(first_inv_ref[...], jnp.concatenate([high, low, high], 0))
            for offset in range(2):
                for chunk in range(chunks):
                    send_ref[pl.ds((column + offset) * rows + signal * chunks + chunk, blocks, stride=stride), :] = result[
                        chunk * blocks : (chunk + 1) * blocks, offset * LANES : (offset + 1) * LANES
                    ]


def fill_kernel(blocks, chunks, count, conv_ref, *refs):
    columns = 2 * chunks
    rows = 3 * chunks
    total = refs[0][...]
    for ref in refs[1:count]:
        total = total + ref[...]
    send_ref = refs[count]
    for place in range(blocks * columns):
        send_ref[pl.ds(place * rows, 2 * chunks), :] = conv_ref[pl.ds(place * 2 * chunks, 2 * chunks), :]
    for chunk in range(chunks):
        piece = total[chunk * blocks : (chunk + 1) * blocks, :]
        for column in range(columns):
            send_ref[pl.ds(column * rows + 2 * chunks + chunk, blocks, stride=columns * rows), :] = piece


def output_kernel(
    chunks, scale, recv_ref, query_ref, key_ref, value_ref, cotangent_ref,
    gated_ref, grad_query_ref, grad_key_ref, grad_value_ref, grad_taps_ref,
):
    rows = 3 * chunks
    for chunk in range(chunks):
        part = pl.ds(chunk * LANES, LANES)
        conv = recv_ref[pl.ds(chunk, LANES, stride=rows), :].T
        gated_ref[part, :] = (query_ref[part, :].astype(jnp.float32) * conv).astype(jnp.bfloat16)
        grad_query_ref[part, :] = (cotangent_ref[part, :].astype(jnp.float32) * conv).astype(jnp.bfloat16)
        grad_gate = recv_ref[pl.ds(chunks + chunk, LANES, stride=rows), :].T
        grad_key_ref[part, :] = (grad_gate * value_ref[part, :].astype(jnp.float32)).astype(jnp.bfloat16)
        grad_value_ref[part, :] = (grad_gate * key_ref[part, :].astype(jnp.float32)).astype(jnp.bfloat16)
        grad_taps_ref[part, :] = recv_ref[pl.ds(2 * chunks + chunk, LANES, stride=rows), :].T * scale


def params():
    return pltpu.CompilerParams(vmem_limit_bytes=48 * 1024 * 1024)


def whole(count):
    return [pl.BlockSpec(memory_space=pltpu.VMEM)] * count


def pack(place, query, key, value, taps, cotangent):
    length = query.shape[0]
    chunks = length // LANES
    wide = pltpu.VMEM((length, LANES), jnp.bfloat16)
    return pl.pallas_call(
        lambda *refs: pack_kernel(chunks, *refs),
        out_shape=jax.ShapeDtypeStruct((LANES * (2 * chunks + 1), LANES), jnp.float32),
        in_specs=[pl.BlockSpec(memory_space=pltpu.SMEM)] + [pl.BlockSpec(memory_space=pltpu.HBM)] * 5,
        out_specs=whole(1)[0],
        scratch_shapes=[wide, wide, wide, pltpu.VMEM((LANES, LANES), jnp.float32), wide, pltpu.SemaphoreType.DMA((5,))],
        compiler_params=params(),
        name="pack",
    )(place, *(pltpu.with_memory_space_constraint(array, pltpu.HBM) for array in (query, key, value, taps, cotangent)))


def forward(blocks, chunks, recv, first_fwd, twist, second_fwd, second_inv, first_inv):
    first = blocks * chunks
    count = 4 * chunks * first
    return pl.pallas_call(
        lambda *refs: forward_kernel(blocks, chunks, *refs),
        out_shape=(
            jax.ShapeDtypeStruct((count, 2 * LANES), jnp.float32),
            jax.ShapeDtypeStruct((first, LANES), jnp.float32),
        ),
        in_specs=whole(6),
        out_specs=tuple(whole(2)),
        scratch_shapes=[pltpu.VMEM((count, 2 * LANES), jnp.bfloat16)] * 2,
        compiler_params=params(),
        name="forward",
    )(recv, first_fwd, twist, second_fwd, second_inv, first_inv)


def inverse(blocks, chunks, recv, spec, first_fwd, twist, second_fwd, second_inv, first_inv):
    count = 4 * chunks * blocks * chunks
    return pl.pallas_call(
        lambda *refs: inverse_kernel(blocks, chunks, *refs),
        out_shape=jax.ShapeDtypeStruct((LANES * 2 * chunks, LANES), jnp.float32),
        in_specs=whole(7),
        out_specs=whole(1)[0],
        scratch_shapes=[pltpu.VMEM((count, 2 * LANES), jnp.bfloat16)] * 2,
        compiler_params=params(),
        cost_estimate=pl.CostEstimate(flops=10**9, bytes_accessed=4 * 10**6, transcendentals=0),
        name="inverse",
    )(recv, spec, first_fwd, twist, second_fwd, second_inv, first_inv)


def fill(blocks, chunks, send, *terms):
    return pl.pallas_call(
        lambda *refs: fill_kernel(blocks, chunks, len(terms), *refs),
        out_shape=jax.ShapeDtypeStruct((LANES * 3 * chunks, LANES), jnp.float32),
        in_specs=whole(1 + len(terms)),
        out_specs=whole(1)[0],
        compiler_params=params(),
        name="fill",
    )(send, *terms)


def outputs(scale, recv, query, key, value, cotangent):
    length = query.shape[0]
    chunks = length // LANES
    rows = jax.ShapeDtypeStruct((length, LANES), jnp.bfloat16)
    return pl.pallas_call(
        lambda *refs: output_kernel(chunks, scale, *refs),
        out_shape=(rows, rows, rows, rows, jax.ShapeDtypeStruct((length, LANES), jnp.float32)),
        in_specs=whole(5),
        out_specs=tuple(whole(5)),
        compiler_params=params(),
        name="outputs",
    )(recv, query, key, value, cotangent)


def by_core(*pairs):
    return [(2 * a + core, 2 * b + core) for core in range(2) for a, b in pairs[core]]


def exchange(rows):
    shape = rows.shape
    flat = rows.reshape(LANES, 1, -1)
    return lax.all_to_all(flat, GROUP, 0, 0, tiled=True).reshape(shape)


def on_device(query, key, value, taps, cotangent):
    blocks = lax.axis_size("ctx")
    length = query.shape[0]
    chunks = length // LANES
    first_fwd, twist, second_fwd, second_inv, first_inv = (
        jnp.asarray(table) for table in dft_tables(blocks, chunks)
    )
    place = lax.axis_index(("y", "core")).astype(jnp.int32).reshape(1)
    recv = exchange(pack(place, query, key, value, taps, cotangent))
    spec, terms = forward(blocks, chunks, recv, first_fwd, twist, second_fwd, second_inv, first_inv)
    send = inverse(blocks, chunks, recv, spec, first_fwd, twist, second_fwd, second_inv, first_inv)
    terms = terms + lax.ppermute(terms, ("zh", "core"), by_core(PAIRS_NEAR, PAIRS_ROUND))
    send = fill(blocks, chunks, send, terms, lax.ppermute(terms, ("zh", "core"), by_core(PAIRS_ROUND, PAIRS_NEAR)))
    back = exchange(send)
    scale = 1.0 / math.sqrt(float(blocks * length * lax.axis_size(("y", "zh", "core"))))
    return outputs(scale, back, query, key, value, cotangent)


def solution(mesh):
    split_mesh = Mesh(mesh.devices.reshape(mesh.shape["ctx"], 4, 4, 2), ("ctx", "y", "zh", "core"))
    tp = ("y", "zh", "core")
    wide = P("ctx", tp)
    return jax.shard_map(
        on_device,
        mesh=split_mesh,
        in_specs=(wide, wide, wide, P("ctx", None), wide),
        out_specs=(wide, wide, wide, wide, P("ctx", None)),
        check_vma=False,
    )
```

```python
import math

import numpy as np
import ml_dtypes
import jax
import jax.numpy as jnp
from jax import lax
from jax.experimental import pallas as pl
from jax.experimental.pallas import tpu as pltpu
from jax.sharding import Mesh, PartitionSpec as P

LANES = 128
GROUP = ("ctx", "y", "core")
PAIRS_NEAR = [(0, 1), (1, 0), (2, 3), (3, 2)]
PAIRS_ROUND = [(0, 3), (3, 0), (1, 2), (2, 1)]


def split_const(table):
    high = table.astype(ml_dtypes.bfloat16)
    low = (table - high.astype(np.float64)).astype(ml_dtypes.bfloat16)
    return high, low


def dft_tables(blocks, chunks):
    first = blocks * chunks
    full = first * LANES
    order = (np.arange(blocks)[None, :] * chunks + np.arange(chunks)[:, None]).reshape(-1)
    k1 = np.arange(first)
    n2 = np.arange(LANES)
    angle = -2 * np.pi * (k1[:, None] * order[None, :] % first) / first + np.pi * order[None, :] / (2 * first)
    first_fwd = np.concatenate([np.cos(angle), np.sin(angle)], 0)
    high, low = split_const(first_fwd)
    first_fwd = np.concatenate([high, high, low], 1)
    high, low = split_const(np.concatenate([np.cos(angle).T, np.sin(angle).T], 1) / full)
    first_inv = np.concatenate([high, high, low], 1)
    angle = -2 * np.pi * (k1[:, None] * n2[None, :]) / full + np.pi * n2[None, :] / (2 * full)
    twist = np.concatenate([np.cos(angle), np.sin(angle)], 1).astype(np.float32)
    angle = 2 * np.pi * (n2[:, None] * n2[None, :] % LANES) / LANES
    cosine, sine = np.cos(angle), np.sin(angle)
    second = np.block([[cosine, -sine], [sine, cosine]])
    second_fwd = np.concatenate(split_const(second), 0)
    second_inv = np.concatenate(split_const(second.T), 0)
    return first_fwd, twist, second_fwd, second_inv, first_inv


def split(values):
    high = values.astype(jnp.bfloat16)
    return high, (values - high.astype(jnp.float32)).astype(jnp.bfloat16)


def dot(left, right):
    return jnp.dot(left, right, preferred_element_type=jnp.float32)


def second_stage(high, low, table):
    table_high = table[: 2 * LANES, :]
    table_low = table[2 * LANES :, :]
    return dot(high, table_high) + dot(low, table_high) + dot(high, table_low)


def pack_kernel(
    chunks, place_ref, query_hbm, key_hbm, value_hbm, taps_hbm, cotangent_hbm, send_ref,
    query_ref, key_ref, value_ref, taps_ref, cotangent_ref, done_ref,
):
    rows = 2 * chunks + 1
    place = place_ref[0]
    start = pl.multiple_of(lax.div(place, 2) * LANES, LANES)
    pairs = (
        (key_hbm, key_ref),
        (value_hbm, value_ref),
        (query_hbm, query_ref),
        (cotangent_hbm, cotangent_ref),
        (taps_hbm.at[pl.ds(start, LANES), :], taps_ref),
    )
    copies = [pltpu.make_async_copy(source, target, done_ref.at[n]) for n, (source, target) in enumerate(pairs)]
    for copy in copies:
        copy.start()
    copies[0].wait()
    copies[1].wait()
    for chunk in range(chunks):
        part = pl.ds(chunk * LANES, LANES)
        gate = key_ref[part, :].astype(jnp.float32) * value_ref[part, :].astype(jnp.float32)
        send_ref[pl.ds(chunk, LANES, stride=rows), :] = gate.T
    copies[2].wait()
    copies[3].wait()
    for chunk in range(chunks):
        part = pl.ds(chunk * LANES, LANES)
        grad = query_ref[part, :].astype(jnp.float32) * cotangent_ref[part, :].astype(jnp.float32)
        send_ref[pl.ds(chunks + chunk, LANES, stride=rows), :] = grad.T
    copies[4].wait()
    lane = lax.broadcasted_iota(jnp.int32, (LANES, LANES), 1)
    mine = lax.div(lane, LANES // 2) == lax.rem(place, 2)
    send_ref[pl.ds(2 * chunks, LANES, stride=rows), :] = jnp.where(mine, taps_ref[...].T, 0.0)


def forward_kernel(
    blocks, chunks, recv_ref, first_ref, twist_ref, second_ref, inverse_ref, first_inv_ref, spec_ref, terms_ref, high_ref, low_ref
):
    rows = 2 * chunks + 1
    first = blocks * chunks
    columns = 2 * chunks
    stride = columns * rows
    cosine = twist_ref[:, :LANES]
    sine = twist_ref[:, LANES:]

    def read(column, signal):
        return jnp.concatenate(
            [recv_ref[pl.ds(column * rows + signal * chunks + chunk, blocks, stride=stride), :] for chunk in range(chunks)], 0
        )

    signals = [read(column, signal) for signal in range(2) for column in range(columns)]
    for start in range(0, len(signals), 2):
        group = signals[start : start + 2]
        high, low = split(jnp.concatenate(group, 1))
        mixed = dot(first_ref[...], jnp.concatenate([high, low, high], 0))
        for offset in range(len(group)):
            lanes = slice(offset * LANES, (offset + 1) * LANES)
            real, imag = mixed[:first, lanes], mixed[first:, lanes]
            high, low = split(jnp.concatenate([real * cosine - imag * sine, imag * cosine + real * sine], 1))
            place = pl.ds((start + offset) * first, first)
            high_ref[place, :] = high
            low_ref[place, :] = low
        if (start + len(group)) % columns == 0:
            done = pl.ds((start + len(group) - columns) * first, columns * first)
            spec_ref[done, :] = second_stage(high_ref[done, :], low_ref[done, :], second_ref)
    real = jnp.zeros((first, LANES), jnp.float32)
    imag = jnp.zeros((first, LANES), jnp.float32)
    for column in range(columns):
        gate = pl.ds(column * first, first)
        grad = pl.ds((columns + column) * first, first)
        gate_real, gate_imag = spec_ref[gate, :LANES], spec_ref[gate, LANES:]
        grad_real, grad_imag = spec_ref[grad, :LANES], spec_ref[grad, LANES:]
        real = real + grad_real * gate_real + grad_imag * gate_imag
        imag = imag + grad_imag * gate_real - grad_real * gate_imag
    high, low = split(jnp.concatenate([real, imag], 1))
    back = second_stage(high, low, inverse_ref)
    real, imag = back[:, :LANES], back[:, LANES:]
    high, low = split(jnp.concatenate([real * cosine + imag * sine, imag * cosine - real * sine], 0))
    terms_ref[...] = dot(first_inv_ref[...], jnp.concatenate([high, low, high], 0))


def inverse_kernel(
    blocks, chunks, recv_ref, spec_ref, first_ref, twist_ref, second_ref, inverse_ref, first_inv_ref, send_ref, high_ref, low_ref
):
    first = blocks * chunks
    columns = 2 * chunks
    cosine = twist_ref[:, :LANES]
    sine = twist_ref[:, LANES:]
    rows = 2 * chunks + 1
    stride = columns * rows
    taps = jnp.concatenate(
        [
            recv_ref[pl.ds(2 * chunk * rows + rows - 1, blocks, stride=stride), :]
            + recv_ref[pl.ds((2 * chunk + 1) * rows + rows - 1, blocks, stride=stride), :]
            for chunk in range(chunks)
        ],
        0,
    )
    high, low = split(taps)
    mixed = dot(first_ref[...], jnp.concatenate([high, low, high], 0))
    real, imag = mixed[:first, :], mixed[first:, :]
    high, low = split(jnp.concatenate([real * cosine - imag * sine, imag * cosine + real * sine], 1))
    taps_spec = second_stage(high, low, second_ref)
    taps_real, taps_imag = taps_spec[:, :LANES], taps_spec[:, LANES:]
    for column in range(columns):
        place = pl.ds(column * first, first)
        real, imag = spec_ref[place, :LANES], spec_ref[place, LANES:]
        high, low = split(jnp.concatenate([real * taps_real - imag * taps_imag, real * taps_imag + imag * taps_real], 1))
        high_ref[place, :] = high
        low_ref[place, :] = low
        place = pl.ds((columns + column) * first, first)
        real, imag = spec_ref[place, :LANES], spec_ref[place, LANES:]
        high, low = split(jnp.concatenate([real * taps_real + imag * taps_imag, imag * taps_real - real * taps_imag], 1))
        high_ref[place, :] = high
        low_ref[place, :] = low
    rows = 2 * chunks
    stride = columns * rows
    back = second_stage(high_ref[...], low_ref[...], inverse_ref)
    for signal in range(2):
        for column in range(0, columns, 2):
            sides = []
            for offset in range(2):
                begin = (signal * columns + column + offset) * first
                real, imag = back[begin : begin + first, :LANES], back[begin : begin + first, LANES:]
                sides.append(jnp.concatenate([real * cosine + imag * sine, imag * cosine - real * sine], 0))
            high, low = split(jnp.concatenate(sides, 1))
            result = dot(first_inv_ref[...], jnp.concatenate([high, low, high], 0))
            for offset in range(2):
                for chunk in range(chunks):
                    send_ref[pl.ds((column + offset) * rows + signal * chunks + chunk, blocks, stride=stride), :] = result[
                        chunk * blocks : (chunk + 1) * blocks, offset * LANES : (offset + 1) * LANES
                    ]


def fill_kernel(blocks, chunks, count, conv_ref, *refs):
    columns = 2 * chunks
    rows = 3 * chunks
    total = refs[0][...]
    for ref in refs[1:count]:
        total = total + ref[...]
    send_ref = refs[count]
    for place in range(blocks * columns):
        send_ref[pl.ds(place * rows, 2 * chunks), :] = conv_ref[pl.ds(place * 2 * chunks, 2 * chunks), :]
    for chunk in range(chunks):
        piece = total[chunk * blocks : (chunk + 1) * blocks, :]
        for column in range(columns):
            send_ref[pl.ds(column * rows + 2 * chunks + chunk, blocks, stride=columns * rows), :] = piece


def output_kernel(
    chunks, scale, recv_ref, query_ref, key_ref, value_ref, cotangent_ref,
    gated_ref, grad_query_ref, grad_key_ref, grad_value_ref, grad_taps_ref,
):
    rows = 3 * chunks
    for chunk in range(chunks):
        part = pl.ds(chunk * LANES, LANES)
        conv = recv_ref[pl.ds(chunk, LANES, stride=rows), :].T
        gated_ref[part, :] = (query_ref[part, :].astype(jnp.float32) * conv).astype(jnp.bfloat16)
        grad_query_ref[part, :] = (cotangent_ref[part, :].astype(jnp.float32) * conv).astype(jnp.bfloat16)
        grad_gate = recv_ref[pl.ds(chunks + chunk, LANES, stride=rows), :].T
        grad_key_ref[part, :] = (grad_gate * value_ref[part, :].astype(jnp.float32)).astype(jnp.bfloat16)
        grad_value_ref[part, :] = (grad_gate * key_ref[part, :].astype(jnp.float32)).astype(jnp.bfloat16)
        grad_taps_ref[part, :] = recv_ref[pl.ds(2 * chunks + chunk, LANES, stride=rows), :].T * scale


def params():
    return pltpu.CompilerParams(vmem_limit_bytes=48 * 1024 * 1024)


def whole(count):
    return [pl.BlockSpec(memory_space=pltpu.VMEM)] * count


def pack(place, query, key, value, taps, cotangent):
    length = query.shape[0]
    chunks = length // LANES
    wide = pltpu.VMEM((length, LANES), jnp.bfloat16)
    return pl.pallas_call(
        lambda *refs: pack_kernel(chunks, *refs),
        out_shape=jax.ShapeDtypeStruct((LANES * (2 * chunks + 1), LANES), jnp.float32),
        in_specs=[pl.BlockSpec(memory_space=pltpu.SMEM)] + [pl.BlockSpec(memory_space=pltpu.HBM)] * 5,
        out_specs=whole(1)[0],
        scratch_shapes=[wide, wide, wide, pltpu.VMEM((LANES, LANES), jnp.float32), wide, pltpu.SemaphoreType.DMA((5,))],
        compiler_params=params(),
        name="pack",
    )(place, *(pltpu.with_memory_space_constraint(array, pltpu.HBM) for array in (query, key, value, taps, cotangent)))


def forward(blocks, chunks, recv, first_fwd, twist, second_fwd, second_inv, first_inv):
    first = blocks * chunks
    count = 4 * chunks * first
    return pl.pallas_call(
        lambda *refs: forward_kernel(blocks, chunks, *refs),
        out_shape=(
            jax.ShapeDtypeStruct((count, 2 * LANES), jnp.float32),
            jax.ShapeDtypeStruct((first, LANES), jnp.float32),
        ),
        in_specs=whole(6),
        out_specs=tuple(whole(2)),
        scratch_shapes=[pltpu.VMEM((count, 2 * LANES), jnp.bfloat16)] * 2,
        compiler_params=params(),
        name="forward",
    )(recv, first_fwd, twist, second_fwd, second_inv, first_inv)


def inverse(blocks, chunks, recv, spec, first_fwd, twist, second_fwd, second_inv, first_inv):
    count = 4 * chunks * blocks * chunks
    return pl.pallas_call(
        lambda *refs: inverse_kernel(blocks, chunks, *refs),
        out_shape=jax.ShapeDtypeStruct((LANES * 2 * chunks, LANES), jnp.float32),
        in_specs=whole(7),
        out_specs=whole(1)[0],
        scratch_shapes=[pltpu.VMEM((count, 2 * LANES), jnp.bfloat16)] * 2,
        compiler_params=params(),
        cost_estimate=pl.CostEstimate(flops=10**9, bytes_accessed=4 * 10**6, transcendentals=0),
        name="inverse",
    )(recv, spec, first_fwd, twist, second_fwd, second_inv, first_inv)


def fill(blocks, chunks, send, *terms):
    return pl.pallas_call(
        lambda *refs: fill_kernel(blocks, chunks, len(terms), *refs),
        out_shape=jax.ShapeDtypeStruct((LANES * 3 * chunks, LANES), jnp.float32),
        in_specs=whole(1 + len(terms)),
        out_specs=whole(1)[0],
        compiler_params=params(),
        name="fill",
    )(send, *terms)


def outputs(scale, recv, query, key, value, cotangent):
    length = query.shape[0]
    chunks = length // LANES
    rows = jax.ShapeDtypeStruct((length, LANES), jnp.bfloat16)
    return pl.pallas_call(
        lambda *refs: output_kernel(chunks, scale, *refs),
        out_shape=(rows, rows, rows, rows, jax.ShapeDtypeStruct((length, LANES), jnp.float32)),
        in_specs=whole(5),
        out_specs=tuple(whole(5)),
        compiler_params=params(),
        name="outputs",
    )(recv, query, key, value, cotangent)


def by_core(*pairs):
    return [(2 * a + core, 2 * b + core) for core in range(2) for a, b in pairs[core]]


def exchange(rows):
    shape = rows.shape
    flat = rows.reshape(LANES, 1, -1)
    return lax.all_to_all(flat, GROUP, 0, 0, tiled=True).reshape(shape)


def on_device(query, key, value, taps, cotangent):
    blocks = lax.axis_size("ctx")
    length = query.shape[0]
    chunks = length // LANES
    first_fwd, twist, second_fwd, second_inv, first_inv = (
        jnp.asarray(table) for table in dft_tables(blocks, chunks)
    )
    place = lax.axis_index(("y", "core")).astype(jnp.int32).reshape(1)
    recv = exchange(pack(place, query, key, value, taps, cotangent))
    spec, terms = forward(blocks, chunks, recv, first_fwd, twist, second_fwd, second_inv, first_inv)
    send = inverse(blocks, chunks, recv, spec, first_fwd, twist, second_fwd, second_inv, first_inv)
    near = lax.ppermute(terms, ("zh", "core"), by_core(PAIRS_NEAR, PAIRS_ROUND))
    near, send = lax.optimization_barrier((near, send))
    terms = terms + near
    send = fill(blocks, chunks, send, terms, lax.ppermute(terms, ("zh", "core"), by_core(PAIRS_ROUND, PAIRS_NEAR)))
    back = exchange(send)
    scale = 1.0 / math.sqrt(float(blocks * length * lax.axis_size(("y", "zh", "core"))))
    return outputs(scale, back, query, key, value, cotangent)


def solution(mesh):
    split_mesh = Mesh(mesh.devices.reshape(mesh.shape["ctx"], 4, 4, 2), ("ctx", "y", "zh", "core"))
    tp = ("y", "zh", "core")
    wide = P("ctx", tp)
    return jax.shard_map(
        on_device,
        mesh=split_mesh,
        in_specs=(wide, wide, wide, P("ctx", None), wide),
        out_specs=(wide, wide, wide, wide, P("ctx", None)),
        check_vma=False,
    )
```

```python
import math

import numpy as np
import ml_dtypes
import jax
import jax.numpy as jnp
from jax import lax
from jax.experimental import pallas as pl
from jax.experimental.pallas import tpu as pltpu
from jax.sharding import Mesh, PartitionSpec as P

LANES = 128
GROUP = ("ctx", "y", "core")
PAIRS_NEAR = [(0, 1), (1, 0), (2, 3), (3, 2)]
PAIRS_ROUND = [(0, 3), (3, 0), (1, 2), (2, 1)]


def split_const(table):
    high = table.astype(ml_dtypes.bfloat16)
    low = (table - high.astype(np.float64)).astype(ml_dtypes.bfloat16)
    return high, low


def dft_tables(blocks, chunks):
    first = blocks * chunks
    full = first * LANES
    order = (np.arange(blocks)[None, :] * chunks + np.arange(chunks)[:, None]).reshape(-1)
    k1 = np.arange(first)
    n2 = np.arange(LANES)
    angle = -2 * np.pi * (k1[:, None] * order[None, :] % first) / first + np.pi * order[None, :] / (2 * first)
    first_fwd = np.concatenate([np.cos(angle), np.sin(angle)], 0)
    high, low = split_const(first_fwd)
    first_fwd = np.concatenate([high, high, low], 1)
    high, low = split_const(np.concatenate([np.cos(angle).T, np.sin(angle).T], 1) / full)
    first_inv = np.concatenate([high, high, low], 1)
    angle = -2 * np.pi * (k1[:, None] * n2[None, :]) / full + np.pi * n2[None, :] / (2 * full)
    twist = np.concatenate([np.cos(angle), np.sin(angle)], 1).astype(np.float32)
    angle = 2 * np.pi * (n2[:, None] * n2[None, :] % LANES) / LANES
    cosine, sine = np.cos(angle), np.sin(angle)
    second = np.block([[cosine, -sine], [sine, cosine]])
    second_fwd = np.concatenate(split_const(second), 0)
    second_inv = np.concatenate(split_const(second.T), 0)
    return first_fwd, twist, second_fwd, second_inv, first_inv


def split(values):
    high = values.astype(jnp.bfloat16)
    return high, (values - high.astype(jnp.float32)).astype(jnp.bfloat16)


def dot(left, right):
    return jnp.dot(left, right, preferred_element_type=jnp.float32)


def second_stage(high, low, table):
    table_high = table[: 2 * LANES, :]
    table_low = table[2 * LANES :, :]
    return dot(high, table_high) + dot(low, table_high) + dot(high, table_low)


def pack_kernel(
    chunks, place_ref, query_hbm, key_hbm, value_hbm, taps_hbm, cotangent_hbm, send_ref,
    query_ref, key_ref, value_ref, taps_ref, cotangent_ref, done_ref,
):
    rows = 2 * chunks + 1
    place = place_ref[0]
    start = pl.multiple_of(lax.div(place, 2) * LANES, LANES)
    pairs = (
        (key_hbm, key_ref),
        (value_hbm, value_ref),
        (query_hbm, query_ref),
        (cotangent_hbm, cotangent_ref),
        (taps_hbm.at[pl.ds(start, LANES), :], taps_ref),
    )
    copies = [pltpu.make_async_copy(source, target, done_ref.at[n]) for n, (source, target) in enumerate(pairs)]
    for copy in copies:
        copy.start()
    copies[0].wait()
    copies[1].wait()
    for chunk in range(chunks):
        part = pl.ds(chunk * LANES, LANES)
        gate = key_ref[part, :].astype(jnp.float32) * value_ref[part, :].astype(jnp.float32)
        send_ref[pl.ds(chunk, LANES, stride=rows), :] = gate.T
    copies[2].wait()
    copies[3].wait()
    for chunk in range(chunks):
        part = pl.ds(chunk * LANES, LANES)
        grad = query_ref[part, :].astype(jnp.float32) * cotangent_ref[part, :].astype(jnp.float32)
        send_ref[pl.ds(chunks + chunk, LANES, stride=rows), :] = grad.T
    copies[4].wait()
    lane = lax.broadcasted_iota(jnp.int32, (LANES, LANES), 1)
    mine = lax.div(lane, LANES // 2) == lax.rem(place, 2)
    send_ref[pl.ds(2 * chunks, LANES, stride=rows), :] = jnp.where(mine, taps_ref[...].T, 0.0)


def forward_kernel(
    blocks, chunks, recv_ref, first_ref, twist_ref, second_ref, inverse_ref, first_inv_ref, spec_ref, terms_ref, high_ref, low_ref
):
    rows = 2 * chunks + 1
    first = blocks * chunks
    columns = 2 * chunks
    stride = columns * rows
    cosine = twist_ref[:, :LANES]
    sine = twist_ref[:, LANES:]

    def read(column, signal):
        return jnp.concatenate(
            [recv_ref[pl.ds(column * rows + signal * chunks + chunk, blocks, stride=stride), :] for chunk in range(chunks)], 0
        )

    taps = jnp.concatenate(
        [
            recv_ref[pl.ds(2 * chunk * rows + rows - 1, blocks, stride=stride), :]
            + recv_ref[pl.ds((2 * chunk + 1) * rows + rows - 1, blocks, stride=stride), :]
            for chunk in range(chunks)
        ],
        0,
    )
    signals = [read(column, signal) for signal in range(2) for column in range(columns)] + [taps]
    for start in range(0, len(signals), 2):
        group = signals[start : start + 2]
        wide = jnp.concatenate(group, 1) if len(group) > 1 else group[0]
        high, low = split(wide)
        mixed = dot(first_ref[...], jnp.concatenate([high, low, high], 0))
        for offset in range(len(group)):
            lanes = slice(offset * LANES, (offset + 1) * LANES)
            real, imag = mixed[:first, lanes], mixed[first:, lanes]
            high, low = split(jnp.concatenate([real * cosine - imag * sine, imag * cosine + real * sine], 1))
            place = pl.ds((start + offset) * first, first)
            high_ref[place, :] = high
            low_ref[place, :] = low
        if (start + len(group)) % columns == 0 or len(group) == 1:
            begin = start + len(group) - (columns if len(group) > 1 else 1)
            done = pl.ds(begin * first, (start + len(group) - begin) * first)
            spec_ref[done, :] = second_stage(high_ref[done, :], low_ref[done, :], second_ref)
    real = jnp.zeros((first, LANES), jnp.float32)
    imag = jnp.zeros((first, LANES), jnp.float32)
    for column in range(columns):
        gate = pl.ds(column * first, first)
        grad = pl.ds((columns + column) * first, first)
        gate_real, gate_imag = spec_ref[gate, :LANES], spec_ref[gate, LANES:]
        grad_real, grad_imag = spec_ref[grad, :LANES], spec_ref[grad, LANES:]
        real = real + grad_real * gate_real + grad_imag * gate_imag
        imag = imag + grad_imag * gate_real - grad_real * gate_imag
    high, low = split(jnp.concatenate([real, imag], 1))
    back = second_stage(high, low, inverse_ref)
    real, imag = back[:, :LANES], back[:, LANES:]
    high, low = split(jnp.concatenate([real * cosine + imag * sine, imag * cosine - real * sine], 0))
    terms_ref[...] = dot(first_inv_ref[...], jnp.concatenate([high, low, high], 0))


def inverse_kernel(blocks, chunks, spec_ref, twist_ref, inverse_ref, first_inv_ref, send_ref, high_ref, low_ref):
    first = blocks * chunks
    columns = 2 * chunks
    cosine = twist_ref[:, :LANES]
    sine = twist_ref[:, LANES:]
    taps = pl.ds(2 * columns * first, first)
    taps_real, taps_imag = spec_ref[taps, :LANES], spec_ref[taps, LANES:]
    for column in range(columns):
        place = pl.ds(column * first, first)
        real, imag = spec_ref[place, :LANES], spec_ref[place, LANES:]
        high, low = split(jnp.concatenate([real * taps_real - imag * taps_imag, real * taps_imag + imag * taps_real], 1))
        high_ref[place, :] = high
        low_ref[place, :] = low
        place = pl.ds((columns + column) * first, first)
        real, imag = spec_ref[place, :LANES], spec_ref[place, LANES:]
        high, low = split(jnp.concatenate([real * taps_real + imag * taps_imag, imag * taps_real - real * taps_imag], 1))
        high_ref[place, :] = high
        low_ref[place, :] = low
    rows = 2 * chunks
    stride = columns * rows
    back = second_stage(high_ref[...], low_ref[...], inverse_ref)
    for signal in range(2):
        for column in range(0, columns, 2):
            sides = []
            for offset in range(2):
                begin = (signal * columns + column + offset) * first
                real, imag = back[begin : begin + first, :LANES], back[begin : begin + first, LANES:]
                sides.append(jnp.concatenate([real * cosine + imag * sine, imag * cosine - real * sine], 0))
            high, low = split(jnp.concatenate(sides, 1))
            result = dot(first_inv_ref[...], jnp.concatenate([high, low, high], 0))
            for offset in range(2):
                for chunk in range(chunks):
                    send_ref[pl.ds((column + offset) * rows + signal * chunks + chunk, blocks, stride=stride), :] = result[
                        chunk * blocks : (chunk + 1) * blocks, offset * LANES : (offset + 1) * LANES
                    ]


def fill_kernel(blocks, chunks, count, conv_ref, *refs):
    columns = 2 * chunks
    rows = 3 * chunks
    total = refs[0][...]
    for ref in refs[1:count]:
        total = total + ref[...]
    send_ref = refs[count]
    for place in range(blocks * columns):
        send_ref[pl.ds(place * rows, 2 * chunks), :] = conv_ref[pl.ds(place * 2 * chunks, 2 * chunks), :]
    for chunk in range(chunks):
        piece = total[chunk * blocks : (chunk + 1) * blocks, :]
        for column in range(columns):
            send_ref[pl.ds(column * rows + 2 * chunks + chunk, blocks, stride=columns * rows), :] = piece


def output_kernel(
    chunks, scale, recv_ref, query_ref, key_ref, value_ref, cotangent_ref,
    gated_ref, grad_query_ref, grad_key_ref, grad_value_ref, grad_taps_ref,
):
    rows = 3 * chunks
    for chunk in range(chunks):
        part = pl.ds(chunk * LANES, LANES)
        conv = recv_ref[pl.ds(chunk, LANES, stride=rows), :].T
        gated_ref[part, :] = (query_ref[part, :].astype(jnp.float32) * conv).astype(jnp.bfloat16)
        grad_query_ref[part, :] = (cotangent_ref[part, :].astype(jnp.float32) * conv).astype(jnp.bfloat16)
        grad_gate = recv_ref[pl.ds(chunks + chunk, LANES, stride=rows), :].T
        grad_key_ref[part, :] = (grad_gate * value_ref[part, :].astype(jnp.float32)).astype(jnp.bfloat16)
        grad_value_ref[part, :] = (grad_gate * key_ref[part, :].astype(jnp.float32)).astype(jnp.bfloat16)
        grad_taps_ref[part, :] = recv_ref[pl.ds(2 * chunks + chunk, LANES, stride=rows), :].T * scale


def params():
    return pltpu.CompilerParams(vmem_limit_bytes=48 * 1024 * 1024)


def whole(count):
    return [pl.BlockSpec(memory_space=pltpu.VMEM)] * count


def pack(place, query, key, value, taps, cotangent):
    length = query.shape[0]
    chunks = length // LANES
    wide = pltpu.VMEM((length, LANES), jnp.bfloat16)
    return pl.pallas_call(
        lambda *refs: pack_kernel(chunks, *refs),
        out_shape=jax.ShapeDtypeStruct((LANES * (2 * chunks + 1), LANES), jnp.float32),
        in_specs=[pl.BlockSpec(memory_space=pltpu.SMEM)] + [pl.BlockSpec(memory_space=pltpu.HBM)] * 5,
        out_specs=whole(1)[0],
        scratch_shapes=[wide, wide, wide, pltpu.VMEM((LANES, LANES), jnp.float32), wide, pltpu.SemaphoreType.DMA((5,))],
        compiler_params=params(),
        name="pack",
    )(place, *(pltpu.with_memory_space_constraint(array, pltpu.HBM) for array in (query, key, value, taps, cotangent)))


def forward(blocks, chunks, recv, first_fwd, twist, second_fwd, second_inv, first_inv):
    first = blocks * chunks
    count = (4 * chunks + 1) * first
    return pl.pallas_call(
        lambda *refs: forward_kernel(blocks, chunks, *refs),
        out_shape=(
            jax.ShapeDtypeStruct((count, 2 * LANES), jnp.float32),
            jax.ShapeDtypeStruct((first, LANES), jnp.float32),
        ),
        in_specs=whole(6),
        out_specs=tuple(whole(2)),
        scratch_shapes=[pltpu.VMEM((count, 2 * LANES), jnp.bfloat16)] * 2,
        compiler_params=params(),
        name="forward",
    )(recv, first_fwd, twist, second_fwd, second_inv, first_inv)


def inverse(blocks, chunks, spec, twist, second_inv, first_inv):
    count = 4 * chunks * blocks * chunks
    return pl.pallas_call(
        lambda *refs: inverse_kernel(blocks, chunks, *refs),
        out_shape=jax.ShapeDtypeStruct((LANES * 2 * chunks, LANES), jnp.float32),
        in_specs=whole(4),
        out_specs=whole(1)[0],
        scratch_shapes=[pltpu.VMEM((count, 2 * LANES), jnp.bfloat16)] * 2,
        compiler_params=params(),
        cost_estimate=pl.CostEstimate(flops=10**9, bytes_accessed=4 * 10**6, transcendentals=0),
        name="inverse",
    )(spec, twist, second_inv, first_inv)


def fill(blocks, chunks, send, *terms):
    return pl.pallas_call(
        lambda *refs: fill_kernel(blocks, chunks, len(terms), *refs),
        out_shape=jax.ShapeDtypeStruct((LANES * 3 * chunks, LANES), jnp.float32),
        in_specs=whole(1 + len(terms)),
        out_specs=whole(1)[0],
        compiler_params=params(),
        name="fill",
    )(send, *terms)


def outputs(scale, recv, query, key, value, cotangent):
    length = query.shape[0]
    chunks = length // LANES
    rows = jax.ShapeDtypeStruct((length, LANES), jnp.bfloat16)
    return pl.pallas_call(
        lambda *refs: output_kernel(chunks, scale, *refs),
        out_shape=(rows, rows, rows, rows, jax.ShapeDtypeStruct((length, LANES), jnp.float32)),
        in_specs=whole(5),
        out_specs=tuple(whole(5)),
        compiler_params=params(),
        name="outputs",
    )(recv, query, key, value, cotangent)


def by_core(*pairs):
    return [(2 * a + core, 2 * b + core) for core in range(2) for a, b in pairs[core]]


def exchange(rows):
    shape = rows.shape
    flat = rows.reshape(LANES, 1, -1)
    return lax.all_to_all(flat, GROUP, 0, 0, tiled=True).reshape(shape)


def on_device(query, key, value, taps, cotangent):
    blocks = lax.axis_size("ctx")
    length = query.shape[0]
    chunks = length // LANES
    first_fwd, twist, second_fwd, second_inv, first_inv = (
        jnp.asarray(table) for table in dft_tables(blocks, chunks)
    )
    place = lax.axis_index(("y", "core")).astype(jnp.int32).reshape(1)
    recv = exchange(pack(place, query, key, value, taps, cotangent))
    spec, terms = forward(blocks, chunks, recv, first_fwd, twist, second_fwd, second_inv, first_inv)
    send = inverse(blocks, chunks, spec, twist, second_inv, first_inv)
    near = lax.ppermute(terms, ("zh", "core"), by_core(PAIRS_NEAR, PAIRS_ROUND))
    near, send = lax.optimization_barrier((near, send))
    terms = terms + near
    send = fill(blocks, chunks, send, terms, lax.ppermute(terms, ("zh", "core"), by_core(PAIRS_ROUND, PAIRS_NEAR)))
    back = exchange(send)
    scale = 1.0 / math.sqrt(float(blocks * length * lax.axis_size(("y", "zh", "core"))))
    return outputs(scale, back, query, key, value, cotangent)


def solution(mesh):
    split_mesh = Mesh(mesh.devices.reshape(mesh.shape["ctx"], 4, 4, 2), ("ctx", "y", "zh", "core"))
    tp = ("y", "zh", "core")
    wide = P("ctx", tp)
    return jax.shard_map(
        on_device,
        mesh=split_mesh,
        in_specs=(wide, wide, wide, P("ctx", None), wide),
        out_specs=(wide, wide, wide, wide, P("ctx", None)),
        check_vma=False,
    )
```

```python
import math

import numpy as np
import ml_dtypes
import jax
import jax.numpy as jnp
from jax import lax
from jax.experimental import pallas as pl
from jax.experimental.pallas import tpu as pltpu
from jax.sharding import Mesh, PartitionSpec as P

LANES = 128
GROUP = ("ctx", "y", "core")
PAIRS_NEAR = [(0, 1), (1, 0), (2, 3), (3, 2)]
PAIRS_ROUND = [(0, 3), (3, 0), (1, 2), (2, 1)]


def split_const(table):
    high = table.astype(ml_dtypes.bfloat16)
    low = (table - high.astype(np.float64)).astype(ml_dtypes.bfloat16)
    return high, low


def dft_tables(blocks, chunks):
    first = blocks * chunks
    full = first * LANES
    order = (np.arange(blocks)[None, :] * chunks + np.arange(chunks)[:, None]).reshape(-1)
    k1 = np.arange(first)
    n2 = np.arange(LANES)
    angle = -2 * np.pi * (k1[:, None] * order[None, :] % first) / first + np.pi * order[None, :] / (2 * first)
    first_fwd = np.concatenate([np.cos(angle), np.sin(angle)], 0)
    high, low = split_const(first_fwd)
    first_fwd = np.concatenate([high, high, low], 1)
    high, low = split_const(np.concatenate([np.cos(angle).T, np.sin(angle).T], 1) / full)
    first_inv = np.concatenate([high, high, low], 1)
    angle = -2 * np.pi * (k1[:, None] * n2[None, :]) / full + np.pi * n2[None, :] / (2 * full)
    twist = np.concatenate([np.cos(angle), np.sin(angle)], 1).astype(np.float32)
    angle = 2 * np.pi * (n2[:, None] * n2[None, :] % LANES) / LANES
    cosine, sine = np.cos(angle), np.sin(angle)
    second = np.block([[cosine, -sine], [sine, cosine]])
    second_fwd = np.concatenate(split_const(second), 0)
    second_inv = np.concatenate(split_const(second.T), 0)
    return first_fwd, twist, second_fwd, second_inv, first_inv


def split(values):
    high = values.astype(jnp.bfloat16)
    return high, (values - high.astype(jnp.float32)).astype(jnp.bfloat16)


def dot(left, right):
    return jnp.dot(left, right, preferred_element_type=jnp.float32)


def second_stage(high, low, table):
    table_high = table[: 2 * LANES, :]
    table_low = table[2 * LANES :, :]
    return dot(high, table_high) + dot(low, table_high) + dot(high, table_low)


def pack_kernel(
    chunks, place_ref, query_hbm, key_hbm, value_hbm, taps_hbm, cotangent_hbm, send_ref,
    query_ref, key_ref, value_ref, taps_ref, cotangent_ref, done_ref,
):
    rows = 2 * chunks + 1
    place = place_ref[0]
    start = pl.multiple_of(lax.div(place, 2) * LANES, LANES)
    pairs = (
        (key_hbm, key_ref),
        (value_hbm, value_ref),
        (query_hbm, query_ref),
        (cotangent_hbm, cotangent_ref),
        (taps_hbm.at[pl.ds(start, LANES), :], taps_ref),
    )
    copies = [pltpu.make_async_copy(source, target, done_ref.at[n]) for n, (source, target) in enumerate(pairs)]
    for copy in copies:
        copy.start()
    copies[0].wait()
    copies[1].wait()
    for chunk in range(chunks):
        part = pl.ds(chunk * LANES, LANES)
        gate = key_ref[part, :].astype(jnp.float32) * value_ref[part, :].astype(jnp.float32)
        send_ref[pl.ds(chunk, LANES, stride=rows), :] = gate.T
    copies[2].wait()
    copies[3].wait()
    for chunk in range(chunks):
        part = pl.ds(chunk * LANES, LANES)
        grad = query_ref[part, :].astype(jnp.float32) * cotangent_ref[part, :].astype(jnp.float32)
        send_ref[pl.ds(chunks + chunk, LANES, stride=rows), :] = grad.T
    copies[4].wait()
    lane = lax.broadcasted_iota(jnp.int32, (LANES, LANES), 1)
    mine = lax.div(lane, LANES // 2) == lax.rem(place, 2)
    send_ref[pl.ds(2 * chunks, LANES, stride=rows), :] = jnp.where(mine, taps_ref[...].T, 0.0)


def forward_kernel(
    blocks, chunks, recv_ref, first_ref, twist_ref, second_ref, inverse_ref, first_inv_ref, spec_ref, terms_ref, high_ref, low_ref
):
    rows = 2 * chunks + 1
    first = blocks * chunks
    columns = 2 * chunks
    stride = columns * rows
    cosine = twist_ref[:, :LANES]
    sine = twist_ref[:, LANES:]

    def read(column, signal):
        return jnp.concatenate(
            [recv_ref[pl.ds(column * rows + signal * chunks + chunk, blocks, stride=stride), :] for chunk in range(chunks)], 0
        )

    taps = jnp.concatenate(
        [
            recv_ref[pl.ds(2 * chunk * rows + rows - 1, blocks, stride=stride), :]
            + recv_ref[pl.ds((2 * chunk + 1) * rows + rows - 1, blocks, stride=stride), :]
            for chunk in range(chunks)
        ],
        0,
    )
    signals = [read(column, signal) for signal in range(2) for column in range(columns)] + [taps]
    for start in range(0, len(signals), 4):
        group = signals[start : start + 4]
        wide = jnp.concatenate(group, 1) if len(group) > 1 else group[0]
        high, low = split(wide)
        mixed = dot(first_ref[...], jnp.concatenate([high, low, high], 0))
        for offset in range(len(group)):
            lanes = slice(offset * LANES, (offset + 1) * LANES)
            real, imag = mixed[:first, lanes], mixed[first:, lanes]
            high, low = split(jnp.concatenate([real * cosine - imag * sine, imag * cosine + real * sine], 1))
            place = pl.ds((start + offset) * first, first)
            high_ref[place, :] = high
            low_ref[place, :] = low
        if (start + len(group)) % columns == 0 or len(group) == 1:
            begin = start + len(group) - (columns if len(group) > 1 else 1)
            done = pl.ds(begin * first, (start + len(group) - begin) * first)
            spec_ref[done, :] = second_stage(high_ref[done, :], low_ref[done, :], second_ref)
    real = jnp.zeros((first, LANES), jnp.float32)
    imag = jnp.zeros((first, LANES), jnp.float32)
    for column in range(columns):
        gate = pl.ds(column * first, first)
        grad = pl.ds((columns + column) * first, first)
        gate_real, gate_imag = spec_ref[gate, :LANES], spec_ref[gate, LANES:]
        grad_real, grad_imag = spec_ref[grad, :LANES], spec_ref[grad, LANES:]
        real = real + grad_real * gate_real + grad_imag * gate_imag
        imag = imag + grad_imag * gate_real - grad_real * gate_imag
    high, low = split(jnp.concatenate([real, imag], 1))
    back = second_stage(high, low, inverse_ref)
    real, imag = back[:, :LANES], back[:, LANES:]
    high, low = split(jnp.concatenate([real * cosine + imag * sine, imag * cosine - real * sine], 0))
    terms_ref[...] = dot(first_inv_ref[...], jnp.concatenate([high, low, high], 0))


def inverse_kernel(blocks, chunks, spec_ref, twist_ref, inverse_ref, first_inv_ref, send_ref, high_ref, low_ref):
    first = blocks * chunks
    columns = 2 * chunks
    cosine = twist_ref[:, :LANES]
    sine = twist_ref[:, LANES:]
    taps = pl.ds(2 * columns * first, first)
    taps_real, taps_imag = spec_ref[taps, :LANES], spec_ref[taps, LANES:]
    for column in range(columns):
        place = pl.ds(column * first, first)
        real, imag = spec_ref[place, :LANES], spec_ref[place, LANES:]
        high, low = split(jnp.concatenate([real * taps_real - imag * taps_imag, real * taps_imag + imag * taps_real], 1))
        high_ref[place, :] = high
        low_ref[place, :] = low
        place = pl.ds((columns + column) * first, first)
        real, imag = spec_ref[place, :LANES], spec_ref[place, LANES:]
        high, low = split(jnp.concatenate([real * taps_real + imag * taps_imag, imag * taps_real - real * taps_imag], 1))
        high_ref[place, :] = high
        low_ref[place, :] = low
    rows = 2 * chunks
    stride = columns * rows
    back = second_stage(high_ref[...], low_ref[...], inverse_ref)
    for signal in range(2):
        for column in range(0, columns, 2):
            sides = []
            for offset in range(2):
                begin = (signal * columns + column + offset) * first
                real, imag = back[begin : begin + first, :LANES], back[begin : begin + first, LANES:]
                sides.append(jnp.concatenate([real * cosine + imag * sine, imag * cosine - real * sine], 0))
            high, low = split(jnp.concatenate(sides, 1))
            result = dot(first_inv_ref[...], jnp.concatenate([high, low, high], 0))
            for offset in range(2):
                for chunk in range(chunks):
                    send_ref[pl.ds((column + offset) * rows + signal * chunks + chunk, blocks, stride=stride), :] = result[
                        chunk * blocks : (chunk + 1) * blocks, offset * LANES : (offset + 1) * LANES
                    ]


def fill_kernel(blocks, chunks, count, conv_ref, *refs):
    columns = 2 * chunks
    rows = 3 * chunks
    total = refs[0][...]
    for ref in refs[1:count]:
        total = total + ref[...]
    send_ref = refs[count]
    for place in range(blocks * columns):
        send_ref[pl.ds(place * rows, 2 * chunks), :] = conv_ref[pl.ds(place * 2 * chunks, 2 * chunks), :]
    for chunk in range(chunks):
        piece = total[chunk * blocks : (chunk + 1) * blocks, :]
        for column in range(columns):
            send_ref[pl.ds(column * rows + 2 * chunks + chunk, blocks, stride=columns * rows), :] = piece


def output_kernel(
    chunks, scale, recv_ref, query_ref, key_ref, value_ref, cotangent_ref,
    gated_ref, grad_query_ref, grad_key_ref, grad_value_ref, grad_taps_ref,
):
    rows = 3 * chunks
    for chunk in range(chunks):
        part = pl.ds(chunk * LANES, LANES)
        conv = recv_ref[pl.ds(chunk, LANES, stride=rows), :].T
        gated_ref[part, :] = (query_ref[part, :].astype(jnp.float32) * conv).astype(jnp.bfloat16)
        grad_query_ref[part, :] = (cotangent_ref[part, :].astype(jnp.float32) * conv).astype(jnp.bfloat16)
        grad_gate = recv_ref[pl.ds(chunks + chunk, LANES, stride=rows), :].T
        grad_key_ref[part, :] = (grad_gate * value_ref[part, :].astype(jnp.float32)).astype(jnp.bfloat16)
        grad_value_ref[part, :] = (grad_gate * key_ref[part, :].astype(jnp.float32)).astype(jnp.bfloat16)
        grad_taps_ref[part, :] = recv_ref[pl.ds(2 * chunks + chunk, LANES, stride=rows), :].T * scale


def params():
    return pltpu.CompilerParams(vmem_limit_bytes=48 * 1024 * 1024)


def whole(count):
    return [pl.BlockSpec(memory_space=pltpu.VMEM)] * count


def pack(place, query, key, value, taps, cotangent):
    length = query.shape[0]
    chunks = length // LANES
    wide = pltpu.VMEM((length, LANES), jnp.bfloat16)
    return pl.pallas_call(
        lambda *refs: pack_kernel(chunks, *refs),
        out_shape=jax.ShapeDtypeStruct((LANES * (2 * chunks + 1), LANES), jnp.float32),
        in_specs=[pl.BlockSpec(memory_space=pltpu.SMEM)] + [pl.BlockSpec(memory_space=pltpu.HBM)] * 5,
        out_specs=whole(1)[0],
        scratch_shapes=[wide, wide, wide, pltpu.VMEM((LANES, LANES), jnp.float32), wide, pltpu.SemaphoreType.DMA((5,))],
        compiler_params=params(),
        name="pack",
    )(place, *(pltpu.with_memory_space_constraint(array, pltpu.HBM) for array in (query, key, value, taps, cotangent)))


def forward(blocks, chunks, recv, first_fwd, twist, second_fwd, second_inv, first_inv):
    first = blocks * chunks
    count = (4 * chunks + 1) * first
    return pl.pallas_call(
        lambda *refs: forward_kernel(blocks, chunks, *refs),
        out_shape=(
            jax.ShapeDtypeStruct((count, 2 * LANES), jnp.float32),
            jax.ShapeDtypeStruct((first, LANES), jnp.float32),
        ),
        in_specs=whole(6),
        out_specs=tuple(whole(2)),
        scratch_shapes=[pltpu.VMEM((count, 2 * LANES), jnp.bfloat16)] * 2,
        compiler_params=params(),
        name="forward",
    )(recv, first_fwd, twist, second_fwd, second_inv, first_inv)


def inverse(blocks, chunks, spec, twist, second_inv, first_inv):
    count = 4 * chunks * blocks * chunks
    return pl.pallas_call(
        lambda *refs: inverse_kernel(blocks, chunks, *refs),
        out_shape=jax.ShapeDtypeStruct((LANES * 2 * chunks, LANES), jnp.float32),
        in_specs=whole(4),
        out_specs=whole(1)[0],
        scratch_shapes=[pltpu.VMEM((count, 2 * LANES), jnp.bfloat16)] * 2,
        compiler_params=params(),
        cost_estimate=pl.CostEstimate(flops=10**9, bytes_accessed=4 * 10**6, transcendentals=0),
        name="inverse",
    )(spec, twist, second_inv, first_inv)


def fill(blocks, chunks, send, *terms):
    return pl.pallas_call(
        lambda *refs: fill_kernel(blocks, chunks, len(terms), *refs),
        out_shape=jax.ShapeDtypeStruct((LANES * 3 * chunks, LANES), jnp.float32),
        in_specs=whole(1 + len(terms)),
        out_specs=whole(1)[0],
        compiler_params=params(),
        name="fill",
    )(send, *terms)


def outputs(scale, recv, query, key, value, cotangent):
    length = query.shape[0]
    chunks = length // LANES
    rows = jax.ShapeDtypeStruct((length, LANES), jnp.bfloat16)
    return pl.pallas_call(
        lambda *refs: output_kernel(chunks, scale, *refs),
        out_shape=(rows, rows, rows, rows, jax.ShapeDtypeStruct((length, LANES), jnp.float32)),
        in_specs=whole(5),
        out_specs=tuple(whole(5)),
        compiler_params=params(),
        name="outputs",
    )(recv, query, key, value, cotangent)


def by_core(*pairs):
    return [(2 * a + core, 2 * b + core) for core in range(2) for a, b in pairs[core]]


def exchange(rows):
    shape = rows.shape
    flat = rows.reshape(LANES, 1, -1)
    return lax.all_to_all(flat, GROUP, 0, 0, tiled=True).reshape(shape)


def on_device(query, key, value, taps, cotangent):
    blocks = lax.axis_size("ctx")
    length = query.shape[0]
    chunks = length // LANES
    first_fwd, twist, second_fwd, second_inv, first_inv = (
        jnp.asarray(table) for table in dft_tables(blocks, chunks)
    )
    place = lax.axis_index(("y", "core")).astype(jnp.int32).reshape(1)
    recv = exchange(pack(place, query, key, value, taps, cotangent))
    spec, terms = forward(blocks, chunks, recv, first_fwd, twist, second_fwd, second_inv, first_inv)
    send = inverse(blocks, chunks, spec, twist, second_inv, first_inv)
    terms = terms + lax.ppermute(terms, ("zh", "core"), by_core(PAIRS_NEAR, PAIRS_ROUND))
    send = fill(blocks, chunks, send, terms, lax.ppermute(terms, ("zh", "core"), by_core(PAIRS_ROUND, PAIRS_NEAR)))
    back = exchange(send)
    scale = 1.0 / math.sqrt(float(blocks * length * lax.axis_size(("y", "zh", "core"))))
    return outputs(scale, back, query, key, value, cotangent)


def solution(mesh):
    split_mesh = Mesh(mesh.devices.reshape(mesh.shape["ctx"], 4, 4, 2), ("ctx", "y", "zh", "core"))
    tp = ("y", "zh", "core")
    wide = P("ctx", tp)
    return jax.shard_map(
        on_device,
        mesh=split_mesh,
        in_specs=(wide, wide, wide, P("ctx", None), wide),
        out_specs=(wide, wide, wide, wide, P("ctx", None)),
        check_vma=False,
    )
```
